256 devices in a mesh: fsdp: 16 (over x_lo, z), rep: 16 (over y, x_hi, core).
Axes of the slice: x: 4 (x_hi: 2, x_lo: 2; x = x_hi * 2 + x_lo), y: 4, z: 8, core: 2. Of those that a mesh axis runs over, the one named last changes fastest.
Arguments:
- samples: bfloat16 [6144, 4096], P(('fsdp', 'rep')), may hold values from -10 to 10
- dual_weight: bfloat16 [8192, 4096], P('fsdp'), may hold values from -0.09375 to 0.09375
- dual_vector: float32 [2, 8192], P(None, 'fsdp'), may hold values from 0 to 2
- map_weight: float32 [8192, 4096], P(('fsdp', 'rep')), may hold values from -0.09375 to 0.09375
- map_vector: float32 [2, 8192], P(None, ('fsdp', 'rep')), may hold values from 0.001 to 2
- moment_weight: float32 [8192, 4096], P(('fsdp', 'rep')), may hold values from -0.006 to 0.006
- square_weight: float32 [8192, 4096], P(('fsdp', 'rep')), may hold values from 0.0001 to 0.01
- moment_vector: float32 [2, 8192], P(None, ('fsdp', 'rep')), may hold values from -0.03 to 0.03
- square_vector: float32 [2, 8192], P(None, ('fsdp', 'rep')), may hold values from 0.0001 to 0.01
Outputs:
- next_weight: float32 [8192, 4096], P(('fsdp', 'rep'))
- next_vector: float32 [2, 8192], P(None, ('fsdp', 'rep'))
- next_moment_weight: float32 [8192, 4096], P(('fsdp', 'rep'))
- next_square_weight: float32 [8192, 4096], P(('fsdp', 'rep'))
- next_moment_vector: float32 [2, 8192], P(None, ('fsdp', 'rep'))
- next_square_vector: float32 [2, 8192], P(None, ('fsdp', 'rep'))
The draws below stay inside these ranges and needn't reach their ends.
All inputs are finite; a program needn't handle non-finite values.
Results may differ from the reference program's by a relative error of at most 0.004.
Values may be sent and summed in bfloat16 or wider, within the bound.
No kernel may reach another device: no remote copies, remote signals or barrier semaphores. Data moves between devices by JAX's collectives and lax.ppermute only.
A program may use at most 64 MiB of HBM per device.

```python
import math
import jax
import jax.numpy as jnp
from jax import lax

D = 4096
H = 8192
ROWS = 6144
N_FSDP = 16


def draw_samples(key, part):
    base_key = jax.random.fold_in(key, 11)
    scale_key = jax.random.fold_in(key, 12)
    base = jax.random.truncated_normal(base_key, -4.0, 4.0, (ROWS, D), jnp.float32)
    row_scale = jnp.exp(jax.random.uniform(scale_key, (ROWS, 1), jnp.float32, math.log(0.25), math.log(2.5)))
    return (base * row_scale).astype(jnp.bfloat16)


def steps_of(own_key, dims, cuts, least, high):
    factor_of, own = 1.0, jax.random.fold_in(own_key, 6)
    for dim, shards_of in cuts:
        heights = jnp.exp(jax.random.uniform(jax.random.fold_in(own, dim), (shards_of,), jnp.float32, least / len(cuts), high / len(cuts)))
        factor_of = factor_of * jnp.repeat(heights, dims[dim] // shards_of).reshape([-1 if axis == dim else 1 for axis in range(len(dims))])
    return factor_of


def centred(own_key, shape, deviation, bound, split=(), dtype=jnp.bfloat16):
    values = deviation * jax.random.normal(own_key, shape, jnp.float32)
    if split:
        values = values * steps_of(own_key, shape, split, -0.22, 0.18)
    return jnp.clip(values, -bound, bound).astype(dtype)


def setup_inputs(seed: int = 0) -> dict:
    streams_of = jax.random.split(jax.random.key(seed), 10)
    samples = draw_samples(jax.random.fold_in(streams_of[9], 71), 0)
    dual_weight = centred(streams_of[1], (H, D), D ** -0.5, 0.09375, ((0, 16),))
    dual_vector = jnp.clip(2.0 * jax.random.uniform(streams_of[2], (2, H), jnp.float32) ** steps_of(streams_of[2], (2, H), ((1, 16),), -0.2, 0.2), 0.0, 2.0)
    map_weight = centred(streams_of[3], (H, D), D ** -0.5, 0.09375, ((0, 256),), jnp.float32)
    map_vector = jnp.clip(jnp.exp(math.log(2.0) - 7.6009024 * jax.random.uniform(streams_of[4], (2, H), jnp.float32) ** steps_of(streams_of[4], (2, H), ((1, 256),), -0.2, 0.2)), 0.001, 2.0)
    moment_weight = centred(streams_of[5], (H, D), 0.001, 0.006, ((0, 256),), jnp.float32)
    square_weight = jnp.clip(jnp.exp(math.log(0.01) - 4.6051702 * jax.random.uniform(streams_of[6], (H, D), jnp.float32) ** steps_of(streams_of[6], (H, D), ((0, 256),), -0.2, 0.2)), 0.0001, 0.01)
    moment_vector = centred(streams_of[7], (2, H), 0.005, 0.03, ((1, 256),), jnp.float32)
    square_vector = jnp.clip(jnp.exp(math.log(0.01) - 4.6051702 * jax.random.uniform(streams_of[8], (2, H), jnp.float32) ** steps_of(streams_of[8], (2, H), ((1, 256),), -0.2, 0.2)), 0.0001, 0.01)
    return dict(samples=samples, dual_weight=dual_weight, dual_vector=dual_vector, map_weight=map_weight, map_vector=map_vector, moment_weight=moment_weight, square_weight=square_weight, moment_vector=moment_vector, square_vector=square_vector)


beta_one = 0.9
beta_two = 0.999
learn_rate = 0.001
epsilon = 1e-08
adam_step = 10

def contract_last(left, right):
    return lax.dot_general(left, right, (((1,), (1,)), ((), ())), preferred_element_type=jnp.float32)

def contract_first(left, right):
    return lax.dot_general(left, right, (((0,), (0,)), ((), ())), preferred_element_type=jnp.float32)

def block_sum(left, right):
    block_size = right.shape[0] // N_FSDP
    left_blocks = jnp.transpose(left.reshape(left.shape[0], N_FSDP, block_size), (1, 0, 2))
    right_blocks = right.reshape(N_FSDP, block_size, right.shape[1])

    def add_block(running, pieces):
        partial_sum = jnp.dot(pieces[0], pieces[1], preferred_element_type=jnp.float32)
        rounded = lax.optimization_barrier(partial_sum.astype(jnp.bfloat16)).astype(jnp.float32)
        return (running + rounded, None)
    initial = jnp.zeros((left.shape[0], right.shape[1]), jnp.float32)
    running, _ = lax.scan(add_block, initial, (left_blocks, right_blocks))
    return running

def adam_update(param, grad, moment, square):
    moment_new = beta_one * moment + (1.0 - beta_one) * grad
    square_new = beta_two * square + (1.0 - beta_two) * grad * grad
    fix_one = 1.0 - beta_one ** adam_step
    fix_two = 1.0 - beta_two ** adam_step
    update = learn_rate * (moment_new / fix_one) / (jnp.sqrt(square_new / fix_two) + epsilon)
    return (param - update, moment_new, square_new)

def reference(samples, dual_weight, dual_vector, map_weight, map_vector, moment_weight, square_weight, moment_vector, square_vector):
    weight_low = map_weight.astype(jnp.bfloat16)
    vector_low = lax.optimization_barrier(map_vector.astype(jnp.bfloat16)).astype(jnp.float32)
    readout = vector_low[0]
    offset = vector_low[1]
    sample_float = samples.astype(jnp.float32)
    hidden = contract_last(samples, weight_low) + offset
    sigma = jax.nn.sigmoid(hidden)
    scaled = (readout * sigma).astype(jnp.bfloat16)
    mapped = sample_float + block_sum(scaled, weight_low)
    mapped_low = mapped.astype(jnp.bfloat16)
    dual_hidden = contract_last(mapped_low, dual_weight) + dual_vector[1]
    dual_scaled = (dual_vector[0] * jax.nn.sigmoid(dual_hidden)).astype(jnp.bfloat16)
    dual_grad = mapped + block_sum(dual_scaled, dual_weight)
    residual = (sample_float - dual_grad).astype(jnp.bfloat16)
    pulled = contract_last(residual, weight_low)
    slope = sigma * (1.0 - sigma)
    curve_term = (readout * slope * pulled).astype(jnp.bfloat16)
    inverse_rows = 1.0 / ROWS
    grad_weight = (contract_first(scaled, residual) + contract_first(curve_term, samples)) * inverse_rows
    grad_vector = jnp.stack([lax.optimization_barrier(jnp.sum(sigma * pulled, axis=0)), lax.optimization_barrier(jnp.sum(readout * slope * pulled, axis=0))]) * inverse_rows
    next_weight, next_moment_weight, next_square_weight = adam_update(map_weight, grad_weight, moment_weight, square_weight)
    raw_vector, next_moment_vector, next_square_vector = adam_update(map_vector, grad_vector, moment_vector, square_vector)
    next_vector = jnp.concatenate([jnp.maximum(raw_vector[0:1], 0.0), raw_vector[1:2]], axis=0)
    return (next_weight, next_vector, next_moment_weight, next_square_weight, next_moment_vector, next_square_vector)
```

```python
import jax
import jax.numpy as jnp
from jax import lax
from jax.sharding import Mesh, PartitionSpec as P

beta_one = 0.9
beta_two = 0.999
learn_rate = 0.001
epsilon = 1e-08
adam_step = 10
extra = 128

flip = [(0, 1), (1, 0)]


def contract_last(left, right):
    return lax.dot_general(
        left, right, (((1,), (1,)), ((), ())), preferred_element_type=jnp.float32
    )


def contract_first(left, right):
    return lax.dot_general(
        left, right, (((0,), (0,)), ((), ())), preferred_element_type=jnp.float32
    )


def dot(left, right):
    return jnp.dot(left, right, preferred_element_type=jnp.float32)


def adam_update(param, grad, moment, square):
    moment_new = beta_one * moment + (1.0 - beta_one) * grad
    square_new = beta_two * square + (1.0 - beta_two) * grad * grad
    fix_one = 1.0 - beta_one**adam_step
    fix_two = 1.0 - beta_two**adam_step
    update = learn_rate * (moment_new / fix_one) / (jnp.sqrt(square_new / fix_two) + epsilon)
    return (param - update, moment_new, square_new)


def shift_y(value, step):
    return lax.ppermute(value, "y", [(i, (i + step) % 4) for i in range(4)])


ring_x = (0, 2, 1, 3)


def shift_x(value, step):
    return lax.ppermute(
        value, ("xl", "xh"), [(ring_x[i], ring_x[(i + step) % 4]) for i in range(4)]
    )


def spread(value, shift):
    return jnp.concatenate([value] + [shift(value, step) for step in (1, 2, 3)], axis=0)


def collect(value, shift):
    rows = value.shape[0] // 4
    total = value[:rows].astype(jnp.float32)
    for step in (1, 2, 3):
        piece = shift(value[rows * step : rows * (step + 1)], -step)
        total = total + piece.astype(jnp.float32)
    return total


def other_core(value):
    return lax.ppermute(value, "core", flip)


def body(
    samples,
    dual_weight,
    dual_vector,
    map_weight,
    map_vector,
    moment_weight,
    square_weight,
    moment_vector,
    square_vector,
):
    core = lax.axis_index("core")
    width = samples.shape[1]
    inverse_rows = 1.0 / 6144

    packed = jnp.concatenate(
        [
            map_weight.astype(jnp.bfloat16),
            jnp.pad(map_vector.astype(jnp.bfloat16).T, ((0, 0), (0, extra - 2))),
        ],
        axis=1,
    )
    first = spread(spread(packed[:16], shift_x), shift_y)
    second = spread(spread(packed[16:], shift_y), shift_x)
    slab = jnp.concatenate([first, second], axis=0)
    weight = slab[:, :width]
    readout = slab[:, width].astype(jnp.float32)
    offset = slab[:, width + 1].astype(jnp.float32)

    rows_own = lax.all_gather(samples, "z", axis=0, tiled=True)
    rows_other = other_core(rows_own)

    half = dual_weight.shape[0] // 2
    dual_half = lax.dynamic_slice_in_dim(dual_weight, core * half, half, axis=0)
    dual_small = lax.dynamic_slice_in_dim(dual_vector, core * half, half, axis=1)
    dual_slab = jnp.concatenate([dual_half, lax.ppermute(dual_half, "xl", flip)], axis=0)
    dual_pair = jnp.concatenate([dual_small, lax.ppermute(dual_small, "xl", flip)], axis=1)

    def reduce_rows(left_own, left_other, right):
        sent = other_core(dot(left_other, right).astype(jnp.bfloat16))
        both = dot(left_own, right).astype(jnp.bfloat16).astype(jnp.float32) + sent.astype(
            jnp.float32
        )
        return lax.psum_scatter(
            both.astype(jnp.bfloat16), "z", scatter_dimension=0, tiled=True
        ).astype(jnp.float32)

    sigma_own = jax.nn.sigmoid(contract_last(rows_own, weight) + offset)
    sigma_other = jax.nn.sigmoid(contract_last(rows_other, weight) + offset)
    scaled_own = (readout * sigma_own).astype(jnp.bfloat16)
    scaled_other = (readout * sigma_other).astype(jnp.bfloat16)

    sample_float = samples.astype(jnp.float32)
    mapped = sample_float + reduce_rows(scaled_own, scaled_other, weight)
    low_own = lax.all_gather(mapped.astype(jnp.bfloat16), "z", axis=0, tiled=True)
    low_other = other_core(low_own)

    def dual_of(low):
        hidden = contract_last(low, dual_slab) + dual_pair[1]
        return (dual_pair[0] * jax.nn.sigmoid(hidden)).astype(jnp.bfloat16)

    dual_grad = mapped + reduce_rows(dual_of(low_own), dual_of(low_other), dual_slab)
    residual = (sample_float - dual_grad).astype(jnp.bfloat16)
    residual_own = lax.all_gather(residual, "z", axis=0, tiled=True)
    residual_other = other_core(residual_own)

    def curve_of(sigma, rows):
        pulled = contract_last(rows, weight)
        curve = readout * (sigma * (1.0 - sigma)) * pulled
        sums = jnp.stack([jnp.sum(sigma * pulled, axis=0), jnp.sum(curve, axis=0)], axis=1)
        return curve.astype(jnp.bfloat16), sums

    curve_own, sums_own = curve_of(sigma_own, residual_own)
    curve_other, sums_other = curve_of(sigma_other, residual_other)
    left_stack = jnp.concatenate([scaled_own, scaled_other, curve_own, curve_other], axis=0)
    right_stack = jnp.concatenate(
        [residual_own, residual_other, rows_own, rows_other], axis=0
    )
    grad_slab = (contract_first(left_stack, right_stack) * inverse_rows).astype(jnp.bfloat16)
    grad_small = ((sums_own + sums_other) * inverse_rows).astype(jnp.bfloat16)
    grad = jnp.concatenate(
        [grad_slab, jnp.pad(grad_small, ((0, 0), (0, extra - 2)))], axis=1
    )
    count = grad.shape[0] // 2
    grad_first = collect(collect(grad[:count], shift_y).astype(jnp.bfloat16), shift_x)
    grad_second = collect(collect(grad[count:], shift_x).astype(jnp.bfloat16), shift_y)
    owner = jnp.concatenate([grad_first, grad_second], axis=0)
    owner_weight = owner[:, :width]
    owner_vector = owner[:, width : width + 2].T

    next_weight, next_moment_weight, next_square_weight = adam_update(
        map_weight, owner_weight, moment_weight, square_weight
    )
    raw_vector, next_moment_vector, next_square_vector = adam_update(
        map_vector, owner_vector, moment_vector, square_vector
    )
    next_vector = jnp.concatenate([jnp.maximum(raw_vector[0:1], 0.0), raw_vector[1:2]], axis=0)
    return (
        next_weight,
        next_vector,
        next_moment_weight,
        next_square_weight,
        next_moment_vector,
        next_square_vector,
    )


def solution(mesh):
    fsdp = ("xl", "z")
    rep = ("y", "xh", "core")
    fine = Mesh(mesh.devices.reshape(2, 8, 4, 2, 2), fsdp + rep)
    rows = P(fsdp + rep, None)
    columns = P(None, fsdp + rep)
    return jax.shard_map(
        body,
        mesh=fine,
        in_specs=(rows, P(fsdp, None), P(None, fsdp), rows, columns, rows, rows, columns, columns),
        out_specs=(rows, columns, rows, rows, columns, columns),
        check_vma=False,
    )
```

```python
import jax
import jax.numpy as jnp
from jax import lax
from jax.sharding import Mesh, PartitionSpec as P

beta_one = 0.9
beta_two = 0.999
learn_rate = 0.001
epsilon = 1e-08
adam_step = 10
extra = 128

flip = [(0, 1), (1, 0)]


def contract_last(left, right):
    return lax.dot_general(
        left, right, (((1,), (1,)), ((), ())), preferred_element_type=jnp.float32
    )


def contract_first(left, right):
    return lax.dot_general(
        left, right, (((0,), (0,)), ((), ())), preferred_element_type=jnp.float32
    )


def dot(left, right):
    return jnp.dot(left, right, preferred_element_type=jnp.float32)


def adam_update(param, grad, moment, square):
    moment_new = beta_one * moment + (1.0 - beta_one) * grad
    square_new = beta_two * square + (1.0 - beta_two) * grad * grad
    fix_one = 1.0 - beta_one**adam_step
    fix_two = 1.0 - beta_two**adam_step
    update = learn_rate * (moment_new / fix_one) / (jnp.sqrt(square_new / fix_two) + epsilon)
    return (param - update, moment_new, square_new)


def shift_y(value, step):
    return lax.ppermute(value, "y", [(i, (i + step) % 4) for i in range(4)])


ring_x = (0, 2, 1, 3)


def shift_x(value, step):
    return lax.ppermute(
        value, ("xl", "xh"), [(ring_x[i], ring_x[(i + step) % 4]) for i in range(4)]
    )


def spread(value, shift):
    return jnp.concatenate([value] + [shift(value, step) for step in (1, 2, 3)], axis=0)


def collect(value, shift):
    rows = value.shape[0] // 4
    total = value[:rows].astype(jnp.float32)
    for step in (1, 2, 3):
        piece = shift(value[rows * step : rows * (step + 1)], -step)
        total = total + piece.astype(jnp.float32)
    return total


def other_core(value):
    return lax.ppermute(value, "core", flip)


def shift_z(value, step):
    return lax.ppermute(value, "z", [(i, (i + step) % 8) for i in range(8)])


def gather_z(value):
    middle = value.shape[1] // 2
    from_ahead, from_behind = shift_z(value, -2), shift_z(value, 2)
    next_ahead, next_behind = shift_z(value, -1), shift_z(value, 1)
    left, right = shift_z(from_behind[:, :middle], 2), shift_z(from_ahead[:, middle:], -2)
    third_ahead, third_behind = shift_z(from_ahead, -1), shift_z(from_behind, 1)
    return (
        jnp.concatenate([from_behind, next_behind, value, next_ahead, from_ahead], axis=0),
        jnp.concatenate(
            [third_ahead, jnp.concatenate([left, right], axis=1), third_behind], axis=0
        ),
    )


def reduce_z(near_sum, far_sum):
    wide = jnp.float32
    count = near_sum.shape[0] // 5
    middle = near_sum.shape[1] // 2

    def near_block(index):
        return near_sum[count * (index + 2) : count * (index + 3)]

    third_ahead, fourth, third_behind = (far_sum[count * i : count * (i + 1)] for i in range(3))
    low = jnp.bfloat16
    left = shift_z(fourth[:, :middle].astype(low), 2)
    right = shift_z(fourth[:, middle:].astype(low), -2)
    ahead = shift_z(third_ahead.astype(low), 1)
    behind = shift_z(third_behind.astype(low), -1)
    beside_ahead = shift_z(near_block(1).astype(low), 1)
    beside_behind = shift_z(near_block(-1).astype(low), -1)
    ahead_sum = near_block(2).astype(wide) + ahead.astype(wide)
    behind_sum = near_block(-2).astype(wide) + behind.astype(wide)
    ahead_sum = jnp.concatenate(
        [ahead_sum[:, :middle] + left.astype(wide), ahead_sum[:, middle:]], axis=1
    )
    behind_sum = jnp.concatenate(
        [behind_sum[:, :middle], behind_sum[:, middle:] + right.astype(wide)], axis=1
    )
    from_behind = shift_z(ahead_sum.astype(low), 2)
    from_ahead = shift_z(behind_sum.astype(low), -2)
    total = near_block(0).astype(wide) + beside_ahead.astype(wide) + beside_behind.astype(wide)
    return total + from_behind.astype(wide) + from_ahead.astype(wide)


def body(
    samples,
    dual_weight,
    dual_vector,
    map_weight,
    map_vector,
    moment_weight,
    square_weight,
    moment_vector,
    square_vector,
):
    core = lax.axis_index("core")
    place = lax.axis_index("z")
    count, width = samples.shape
    inverse_rows = 1.0 / 6144

    packed = jnp.concatenate(
        [
            map_weight.astype(jnp.bfloat16),
            jnp.pad(map_vector.astype(jnp.bfloat16).T, ((0, 0), (0, extra - 2))),
        ],
        axis=1,
    )
    first = spread(spread(packed[:16], shift_x), shift_y)
    second = spread(spread(packed[16:], shift_y), shift_x)
    slab = jnp.concatenate([first, second], axis=0)
    weight = slab[:, :width]
    readout = slab[:, width].astype(jnp.float32)
    offset = slab[:, width + 1].astype(jnp.float32)

    rows_all = lax.all_gather(samples, "z", axis=0, tiled=True)
    rows_own = lax.dynamic_slice_in_dim(
        jnp.concatenate([rows_all, rows_all], axis=0), (place + 6) % 8 * count, 8 * count, axis=0
    )
    rows_other = other_core(rows_own)
    cut = 5 * count
    groups = [(rows_own[:cut], rows_other[:cut]), (rows_own[cut:], rows_other[cut:])]

    half = dual_weight.shape[0] // 2
    dual_half = lax.dynamic_slice_in_dim(dual_weight, core * half, half, axis=0)
    dual_small = lax.dynamic_slice_in_dim(dual_vector, core * half, half, axis=1)
    dual_small_received = lax.ppermute(dual_small, "xl", flip)
    dual_small_received, offset = lax.optimization_barrier((dual_small_received, offset))
    dual_slab = jnp.concatenate([dual_half, lax.ppermute(dual_half, "xl", flip)], axis=0)
    dual_pair = jnp.concatenate([dual_small, dual_small_received], axis=1)

    def both_cores(left_own, left_other, right):
        received = other_core(dot(left_other, right).astype(jnp.bfloat16))
        return (dot(left_own, right) + received.astype(jnp.float32)).astype(jnp.bfloat16)

    def sigma_of(rows):
        return jax.nn.sigmoid(contract_last(rows, weight) + offset)

    def scaled_of(sigma):
        return (readout * sigma).astype(jnp.bfloat16)

    sigma_far, sigma_near = (tuple(map(sigma_of, groups[i])) for i in (1, 0))
    scaled_far, scaled_near = tuple(map(scaled_of, sigma_far)), tuple(map(scaled_of, sigma_near))

    sample_float = samples.astype(jnp.float32)
    far_sum = both_cores(*scaled_far, weight)
    near_sum = both_cores(*scaled_near, weight)
    mapped = sample_float + reduce_z(near_sum, far_sum)
    low_near, low_far = gather_z(mapped.astype(jnp.bfloat16))

    def dual_of(low):
        hidden = contract_last(low, dual_slab) + dual_pair[1]
        return (dual_pair[0] * jax.nn.sigmoid(hidden)).astype(jnp.bfloat16)

    def dual_sum(low):
        other = other_core(low)
        return both_cores(dual_of(low), dual_of(other), dual_slab)

    dual_near = dual_sum(low_near)
    dual_far = dual_sum(low_far)
    dual_grad = mapped + reduce_z(dual_near, dual_far)
    residual = (sample_float - dual_grad).astype(jnp.bfloat16)
    residual_near, residual_far = gather_z(residual)

    def curve_of(sigma, rows):
        pulled = contract_last(rows, weight)
        curve = readout * (sigma * (1.0 - sigma)) * pulled
        sums = jnp.stack([jnp.sum(sigma * pulled, axis=0), jnp.sum(curve, axis=0)], axis=1)
        return curve.astype(jnp.bfloat16), sums

    lefts, rights, small = [], [], 0.0
    for sigmas, scaleds, rows, pulled_own in (
        (sigma_near, scaled_near, groups[0], residual_near),
        (sigma_far, scaled_far, groups[1], residual_far),
    ):
        pulled_rows = (pulled_own, other_core(pulled_own))
        for i in range(2):
            curve, sums = curve_of(sigmas[i], pulled_rows[i])
            lefts += [scaleds[i], curve]
            rights += [pulled_rows[i], rows[i]]
            small = small + sums
    left_stack = jnp.concatenate(lefts, axis=0)
    right_stack = jnp.concatenate(rights, axis=0)
    grad_small = jnp.pad(
        (small * inverse_rows).astype(jnp.bfloat16), ((0, 0), (0, extra - 2))
    )

    def grad_part(begin, end):
        part = contract_first(left_stack[:, begin:end], right_stack) * inverse_rows
        return jnp.concatenate([part.astype(jnp.bfloat16), grad_small[begin:end]], axis=1)

    units = left_stack.shape[1]
    grad_first = collect(
        collect(grad_part(0, units // 2), shift_y).astype(jnp.bfloat16), shift_x
    )
    grad_second = collect(
        collect(grad_part(units // 2, units), shift_x).astype(jnp.bfloat16), shift_y
    )
    owner = jnp.concatenate([grad_first, grad_second], axis=0)
    owner_weight = owner[:, :width]
    owner_vector = owner[:, width : width + 2].T

    next_weight, next_moment_weight, next_square_weight = adam_update(
        map_weight, owner_weight, moment_weight, square_weight
    )
    raw_vector, next_moment_vector, next_square_vector = adam_update(
        map_vector, owner_vector, moment_vector, square_vector
    )
    next_vector = jnp.concatenate([jnp.maximum(raw_vector[0:1], 0.0), raw_vector[1:2]], axis=0)
    return (
        next_weight,
        next_vector,
        next_moment_weight,
        next_square_weight,
        next_moment_vector,
        next_square_vector,
    )


def solution(mesh):
    fsdp = ("xl", "z")
    rep = ("y", "xh", "core")
    fine = Mesh(mesh.devices.reshape(2, 8, 4, 2, 2), fsdp + rep)
    rows = P(fsdp + rep, None)
    columns = P(None, fsdp + rep)
    return jax.shard_map(
        body,
        mesh=fine,
        in_specs=(rows, P(fsdp, None), P(None, fsdp), rows, columns, rows, rows, columns, columns),
        out_specs=(rows, columns, rows, rows, columns, columns),
        check_vma=False,
    )
```

```python
import jax
import jax.numpy as jnp
from jax import lax
from jax.experimental import pallas as pl
from jax.experimental.pallas import tpu as pltpu
from jax.sharding import Mesh, PartitionSpec as P

beta_one = 0.9
beta_two = 0.999
learn_rate = 0.001
epsilon = 1e-08
adam_step = 10
extra = 128

flip = [(0, 1), (1, 0)]


def contract_last(left, right):
    return lax.dot_general(
        left, right, (((1,), (1,)), ((), ())), preferred_element_type=jnp.float32
    )


def contract_first(left, right):
    return lax.dot_general(
        left, right, (((0,), (0,)), ((), ())), preferred_element_type=jnp.float32
    )


def dot(left, right):
    return jnp.dot(left, right, preferred_element_type=jnp.float32)


def adam_update(param, grad, moment, square):
    moment_new = beta_one * moment + (1.0 - beta_one) * grad
    square_new = beta_two * square + (1.0 - beta_two) * grad * grad
    fix_one = 1.0 - beta_one**adam_step
    fix_two = 1.0 - beta_two**adam_step
    update = learn_rate * (moment_new / fix_one) / (jnp.sqrt(square_new / fix_two) + epsilon)
    return (param - update, moment_new, square_new)


def shift_y(value, step):
    return lax.ppermute(value, "y", [(i, (i + step) % 4) for i in range(4)])


ring_x = (0, 2, 1, 3)


def shift_x(value, step):
    return lax.ppermute(
        value, ("xl", "xh"), [(ring_x[i], ring_x[(i + step) % 4]) for i in range(4)]
    )


def spread(value, shift):
    return jnp.concatenate([value] + [shift(value, step) for step in (1, 2, 3)], axis=0)


def collect(value, shift):
    rows = value.shape[0] // 4
    total = value[:rows].astype(jnp.float32)
    for step in (1, 2, 3):
        piece = shift(value[rows * step : rows * (step + 1)], -step)
        total = total + piece.astype(jnp.float32)
    return total


def other_core(value):
    return lax.ppermute(value, "core", flip)


def shift_z(value, step):
    return lax.ppermute(value, "z", [(i, (i + step) % 8) for i in range(8)])


def gather_z(value):
    middle = value.shape[1] // 2
    from_ahead, from_behind = shift_z(value, -2), shift_z(value, 2)
    next_ahead, next_behind = shift_z(value, -1), shift_z(value, 1)
    left, right = shift_z(from_behind[:, :middle], 2), shift_z(from_ahead[:, middle:], -2)
    third_ahead, third_behind = shift_z(from_ahead, -1), shift_z(from_behind, 1)
    return (
        jnp.concatenate([from_behind, next_behind, value, next_ahead, from_ahead], axis=0),
        jnp.concatenate(
            [third_ahead, jnp.concatenate([left, right], axis=1), third_behind], axis=0
        ),
    )


def reduce_z(near_sum, far_sum):
    wide = jnp.float32
    count = near_sum.shape[0] // 5
    middle = near_sum.shape[1] // 2

    def near_block(index):
        return near_sum[count * (index + 2) : count * (index + 3)]

    third_ahead, fourth, third_behind = (far_sum[count * i : count * (i + 1)] for i in range(3))
    low = jnp.bfloat16
    left = shift_z(fourth[:, :middle].astype(low), 2)
    right = shift_z(fourth[:, middle:].astype(low), -2)
    ahead = shift_z(third_ahead.astype(low), 1)
    behind = shift_z(third_behind.astype(low), -1)
    beside_ahead = shift_z(near_block(1).astype(low), 1)
    beside_behind = shift_z(near_block(-1).astype(low), -1)
    ahead_sum = near_block(2).astype(wide) + ahead.astype(wide)
    behind_sum = near_block(-2).astype(wide) + behind.astype(wide)
    ahead_sum = jnp.concatenate(
        [ahead_sum[:, :middle] + left.astype(wide), ahead_sum[:, middle:]], axis=1
    )
    behind_sum = jnp.concatenate(
        [behind_sum[:, :middle], behind_sum[:, middle:] + right.astype(wide)], axis=1
    )
    from_behind = shift_z(ahead_sum.astype(low), 2)
    from_ahead = shift_z(behind_sum.astype(low), -2)
    total = near_block(0).astype(wide) + beside_ahead.astype(wide) + beside_behind.astype(wide)
    return total + from_behind.astype(wide) + from_ahead.astype(wide)


tile = 512


def forward_kernel(counts, packed, *refs):
    own_ref, other_ref = refs[:2]
    slabs = refs[2 : 2 + len(counts)]
    refs = refs[2 + len(counts) :]
    if packed:
        tail = slabs[0][:, own_ref.shape[1] :]
        lane = lax.broadcasted_iota(jnp.int32, (8, extra), 1)
        row = lax.broadcasted_iota(jnp.int32, (8, extra), 0)
        pick = jnp.where(lane == row, 1.0, 0.0).astype(jnp.bfloat16)
        vector = contract_last(pick, tail)
        readout, offset = vector[0:1], vector[1:2]
        sum_refs, sigma_refs = refs[0:2], refs[2:4]
        scratch = refs[4:]
    else:
        readout, offset = refs[0][0:1], refs[0][1:2]
        sum_refs, sigma_refs = refs[1:3], None
        scratch = refs[3:]
    width = own_ref.shape[1]
    for index, rows in enumerate((own_ref, other_ref)):
        begin = 0
        for slab, count in zip(slabs, counts):
            for low in range(0, count, 256):
                size = min(256, count - low)
                hidden = contract_last(rows[...], slab[low : low + size, :width])
                span = slice(begin + low, begin + low + size)
                sigma = jax.nn.sigmoid(hidden + offset[:, span])
                if sigma_refs is not None:
                    sigma_refs[index][:, span] = sigma
                scratch[index][:, span] = (readout[:, span] * sigma).astype(jnp.bfloat16)
            begin += count

    @pl.loop(0, width // tile)
    def _(step):
        columns = pl.ds(pl.multiple_of(step * tile, tile), tile)
        for index in (1, 0):
            total, begin = None, 0
            for slab, count in zip(slabs, counts):
                part = dot(scratch[index][:, begin : begin + count], slab[:, columns])
                total = part if total is None else total + part
                begin += count
            sum_refs[index][:, columns] = total.astype(jnp.bfloat16)


def forward(rows_own, rows_other, slabs, vector=None):
    packed = vector is None
    counts = tuple(slab.shape[0] for slab in slabs)
    units = sum(counts)
    count, width = rows_own.shape
    vmem = pl.BlockSpec(memory_space=pltpu.VMEM)
    sums = jax.ShapeDtypeStruct((count, width), jnp.bfloat16)
    sigmas = jax.ShapeDtypeStruct((count, units), jnp.float32)
    outs = (sums, sums) + ((sigmas, sigmas) if packed else ())
    args = (rows_own, rows_other, *slabs) + (() if packed else (vector,))
    return pl.pallas_call(
        lambda *refs: forward_kernel(counts, packed, *refs),
        out_shape=outs,
        in_specs=[vmem] * len(args),
        out_specs=(vmem,) * len(outs),
        scratch_shapes=[pltpu.VMEM((count, units), jnp.bfloat16)] * 2,
        compiler_params=pltpu.CompilerParams(vmem_limit_bytes=40 * 2**20),
        cost_estimate=pl.CostEstimate(
            flops=8 * count * width * units,
            bytes_accessed=2 * width * (4 * count + units),
            transcendentals=2 * count * units,
        ),
    )(*args)


def body(
    samples,
    dual_weight,
    dual_vector,
    map_weight,
    map_vector,
    moment_weight,
    square_weight,
    moment_vector,
    square_vector,
):
    core = lax.axis_index("core")
    place = lax.axis_index("z")
    count, width = samples.shape
    inverse_rows = 1.0 / 6144

    packed = jnp.concatenate(
        [
            map_weight.astype(jnp.bfloat16),
            jnp.pad(map_vector.astype(jnp.bfloat16).T, ((0, 0), (0, extra - 2))),
        ],
        axis=1,
    )
    first = spread(spread(packed[:16], shift_x), shift_y)
    second = spread(spread(packed[16:], shift_y), shift_x)
    slab = jnp.concatenate([first, second], axis=0)
    weight = slab[:, :width]
    readout = slab[:, width].astype(jnp.float32)
    offset = slab[:, width + 1].astype(jnp.float32)

    rows_all = lax.all_gather(samples, "z", axis=0, tiled=True)
    rows_own = lax.dynamic_slice_in_dim(
        jnp.concatenate([rows_all, rows_all], axis=0), (place + 6) % 8 * count, 8 * count, axis=0
    )
    rows_other = other_core(rows_own)
    cut = 5 * count
    groups = [(rows_own[:cut], rows_other[:cut]), (rows_own[cut:], rows_other[cut:])]

    half = dual_weight.shape[0] // 2
    dual_half = lax.dynamic_slice_in_dim(dual_weight, core * half, half, axis=0)
    dual_small = lax.dynamic_slice_in_dim(dual_vector, core * half, half, axis=1)
    dual_small_received = lax.ppermute(dual_small, "xl", flip)
    dual_small_received, slab = lax.optimization_barrier((dual_small_received, slab))
    dual_received = [
        lax.ppermute(dual_half[: half // 2], "xl", flip),
        lax.ppermute(dual_half[half // 2 :], "xl", flip),
    ]
    dual_pair = jnp.concatenate([dual_small, dual_small_received], axis=1)

    sum_own, sum_other, sigma_own, sigma_other = forward(rows_own, rows_other, [slab])
    sigma_near = (sigma_own[:cut], sigma_other[:cut])
    sigma_far = (sigma_own[cut:], sigma_other[cut:])

    def scaled_of(sigma):
        return (readout * sigma).astype(jnp.bfloat16)

    scaled_far, scaled_near = tuple(map(scaled_of, sigma_far)), tuple(map(scaled_of, sigma_near))

    def both_cores(own, other):
        return own.astype(jnp.float32) + other_core(other).astype(jnp.float32)

    sample_float = samples.astype(jnp.float32)
    far_sum = both_cores(sum_own[cut:], sum_other[cut:])
    near_sum = both_cores(sum_own[:cut], sum_other[:cut])
    mapped = sample_float + reduce_z(near_sum, far_sum)
    mapped, dual_received[0] = lax.optimization_barrier((mapped, dual_received[0]))
    low_near, low_far = gather_z(mapped.astype(jnp.bfloat16))
    dual_slabs = [dual_half, *dual_received]

    def dual_sum(low):
        return forward(low, other_core(low), dual_slabs, dual_pair)

    dual_near = dual_sum(low_near)
    dual_near, low_far = lax.optimization_barrier((dual_near, low_far))
    dual_far = dual_sum(low_far)
    dual_far = both_cores(*dual_far)
    dual_grad = mapped + reduce_z(both_cores(*dual_near), dual_far)
    residual = (sample_float - dual_grad).astype(jnp.bfloat16)
    residual_near, residual_far = gather_z(residual)

    def curve_of(sigma, rows):
        pulled = contract_last(rows, weight)
        curve = readout * (sigma * (1.0 - sigma)) * pulled
        sums = jnp.stack([jnp.sum(sigma * pulled, axis=0), jnp.sum(curve, axis=0)], axis=1)
        return curve.astype(jnp.bfloat16), sums

    lefts, rights, small = [], [], 0.0
    for sigmas, scaleds, rows, pulled_own in (
        (sigma_near, scaled_near, groups[0], residual_near),
        (sigma_far, scaled_far, groups[1], residual_far),
    ):
        pulled_rows = (pulled_own, other_core(pulled_own))
        for i in range(2):
            curve, sums = curve_of(sigmas[i], pulled_rows[i])
            lefts += [scaleds[i], curve]
            rights += [pulled_rows[i], rows[i]]
            small = small + sums
    left_stack = jnp.concatenate(lefts, axis=0)
    right_stack = jnp.concatenate(rights, axis=0)
    grad_small = jnp.pad(
        (small * inverse_rows).astype(jnp.bfloat16), ((0, 0), (0, extra - 2))
    )

    def grad_part(begin, end):
        part = contract_first(left_stack[:, begin:end], right_stack) * inverse_rows
        return jnp.concatenate([part.astype(jnp.bfloat16), grad_small[begin:end]], axis=1)

    units = left_stack.shape[1]
    grad_first = collect(
        collect(grad_part(0, units // 2), shift_y).astype(jnp.bfloat16), shift_x
    )
    grad_second = collect(
        collect(grad_part(units // 2, units), shift_x).astype(jnp.bfloat16), shift_y
    )
    owner = jnp.concatenate([grad_first, grad_second], axis=0)
    owner_weight = owner[:, :width]
    owner_vector = owner[:, width : width + 2].T

    next_weight, next_moment_weight, next_square_weight = adam_update(
        map_weight, owner_weight, moment_weight, square_weight
    )
    raw_vector, next_moment_vector, next_square_vector = adam_update(
        map_vector, owner_vector, moment_vector, square_vector
    )
    next_vector = jnp.concatenate([jnp.maximum(raw_vector[0:1], 0.0), raw_vector[1:2]], axis=0)
    return (
        next_weight,
        next_vector,
        next_moment_weight,
        next_square_weight,
        next_moment_vector,
        next_square_vector,
    )


def solution(mesh):
    fsdp = ("xl", "z")
    rep = ("y", "xh", "core")
    fine = Mesh(mesh.devices.reshape(2, 8, 4, 2, 2), fsdp + rep)
    rows = P(fsdp + rep, None)
    columns = P(None, fsdp + rep)
    return jax.shard_map(
        body,
        mesh=fine,
        in_specs=(rows, P(fsdp, None), P(None, fsdp), rows, columns, rows, rows, columns, columns),
        out_specs=(rows, columns, rows, rows, columns, columns),
        check_vma=False,
    )
```

```python
import jax
import jax.numpy as jnp
from jax import lax
from jax.experimental import pallas as pl
from jax.experimental.pallas import tpu as pltpu
from jax.sharding import Mesh, PartitionSpec as P

beta_one = 0.9
beta_two = 0.999
learn_rate = 0.001
epsilon = 1e-08
adam_step = 10
extra = 128

flip = [(0, 1), (1, 0)]


def contract_last(left, right):
    return lax.dot_general(
        left, right, (((1,), (1,)), ((), ())), preferred_element_type=jnp.float32
    )


def contract_first(left, right):
    return lax.dot_general(
        left, right, (((0,), (0,)), ((), ())), preferred_element_type=jnp.float32
    )


def dot(left, right):
    return jnp.dot(left, right, preferred_element_type=jnp.float32)


def adam_update(param, grad, moment, square):
    moment_new = beta_one * moment + (1.0 - beta_one) * grad
    square_new = beta_two * square + (1.0 - beta_two) * grad * grad
    fix_one = 1.0 - beta_one**adam_step
    fix_two = 1.0 - beta_two**adam_step
    update = learn_rate * (moment_new / fix_one) / (jnp.sqrt(square_new / fix_two) + epsilon)
    return (param - update, moment_new, square_new)


def shift_y(value, step):
    return lax.ppermute(value, "y", [(i, (i + step) % 4) for i in range(4)])


ring_x = (0, 2, 1, 3)


def shift_x(value, step):
    return lax.ppermute(
        value, ("xl", "xh"), [(ring_x[i], ring_x[(i + step) % 4]) for i in range(4)]
    )


def spread(value, shift):
    half = value.shape[0] // 2
    behind, ahead = shift(value, 1), shift(value, -1)
    front, back = shift(behind[:half], 1), shift(ahead[half:], -1)
    return jnp.concatenate([value, behind, front, back, ahead], axis=0)


def collect(value, shift):
    wide, low = jnp.float32, jnp.bfloat16
    rows = value.shape[0] // 4
    half = rows // 2
    blocks = [value[rows * i : rows * (i + 1)] for i in range(4)]
    front, back = shift(blocks[2][:half], -1), shift(blocks[2][half:], 1)
    behind = jnp.concatenate(
        [(blocks[1][:half].astype(wide) + front.astype(wide)).astype(low), blocks[1][half:]], axis=0
    )
    ahead = jnp.concatenate(
        [blocks[3][:half], (blocks[3][half:].astype(wide) + back.astype(wide)).astype(low)], axis=0
    )
    return blocks[0].astype(wide) + shift(behind, -1).astype(wide) + shift(ahead, 1).astype(wide)


def other_core(value):
    return lax.ppermute(value, "core", flip)


def shift_z(value, step):
    return lax.ppermute(value, "z", [(i, (i + step) % 8) for i in range(8)])


def gather_z(value, ride=None):
    middle = value.shape[1] // 2
    from_ahead, from_behind = shift_z(value, -2), shift_z(value, 2)
    next_ahead, next_behind = shift_z(value, -1), shift_z(value, 1)
    if ride is not None:
        from_behind, ride = lax.optimization_barrier((from_behind, ride))
    left, right = shift_z(from_behind[:, :middle], 2), shift_z(from_ahead[:, middle:], -2)
    third_ahead, third_behind = shift_z(from_ahead, -1), shift_z(from_behind, 1)
    return (
        jnp.concatenate([from_behind, next_behind, value, next_ahead, from_ahead], axis=0),
        jnp.concatenate(
            [third_ahead, jnp.concatenate([left, right], axis=1), third_behind], axis=0
        ),
        ride,
    )


def reduce_z(near_sum, far_sum, ride=None):
    wide = jnp.float32
    count = near_sum.shape[0] // 5
    middle = near_sum.shape[1] // 2

    def near_block(index):
        return near_sum[count * (index + 2) : count * (index + 3)]

    third_ahead, fourth, third_behind = (far_sum[count * i : count * (i + 1)] for i in range(3))
    low = jnp.bfloat16
    left = shift_z(fourth[:, :middle].astype(low), 2)
    right = shift_z(fourth[:, middle:].astype(low), -2)
    ahead = shift_z(third_ahead.astype(low), 1)
    behind = shift_z(third_behind.astype(low), -1)
    if ride is not None:
        left, ride = lax.optimization_barrier((left, ride))
    beside_ahead = shift_z(near_block(1).astype(low), 1)
    beside_behind = shift_z(near_block(-1).astype(low), -1)
    ahead_sum = near_block(2).astype(wide) + ahead.astype(wide)
    behind_sum = near_block(-2).astype(wide) + behind.astype(wide)
    ahead_sum = jnp.concatenate(
        [ahead_sum[:, :middle] + left.astype(wide), ahead_sum[:, middle:]], axis=1
    )
    behind_sum = jnp.concatenate(
        [behind_sum[:, :middle], behind_sum[:, middle:] + right.astype(wide)], axis=1
    )
    from_behind = shift_z(ahead_sum.astype(low), 2)
    from_ahead = shift_z(behind_sum.astype(low), -2)
    total = near_block(0).astype(wide) + beside_ahead.astype(wide) + beside_behind.astype(wide)
    return total + from_behind.astype(wide) + from_ahead.astype(wide), ride


tile = 512


def forward_kernel(counts, packed, *refs):
    own_ref, other_ref = refs[:2]
    slabs = refs[2 : 2 + len(counts)]
    refs = refs[2 + len(counts) :]
    if packed:
        tail = slabs[0][:, own_ref.shape[1] :]
        lane = lax.broadcasted_iota(jnp.int32, (8, extra), 1)
        row = lax.broadcasted_iota(jnp.int32, (8, extra), 0)
        pick = jnp.where(lane == row, 1.0, 0.0).astype(jnp.bfloat16)
        vector = contract_last(pick, tail)
        readout, offset = vector[0:1], vector[1:2]
        sum_refs, sigma_refs = refs[0:2], refs[2:4]
        scratch = refs[4:]
    else:
        readout, offset = refs[0][0:1], refs[0][1:2]
        sum_refs, sigma_refs = refs[1:3], None
        scratch = refs[3:]
    width = own_ref.shape[1]
    for index, rows in enumerate((own_ref, other_ref)):
        begin = 0
        for slab, count in zip(slabs, counts):
            for low in range(0, count, 256):
                size = min(256, count - low)
                hidden = contract_last(rows[...], slab[low : low + size, :width])
                span = slice(begin + low, begin + low + size)
                sigma = jax.nn.sigmoid(hidden + offset[:, span])
                if sigma_refs is not None:
                    sigma_refs[index][:, span] = sigma
                scratch[index][:, span] = (readout[:, span] * sigma).astype(jnp.bfloat16)
            begin += count

    @pl.loop(0, width // tile)
    def _(step):
        columns = pl.ds(pl.multiple_of(step * tile, tile), tile)
        for index in (1, 0):
            total, begin = None, 0
            for slab, count in zip(slabs, counts):
                part = dot(scratch[index][:, begin : begin + count], slab[:, columns])
                total = part if total is None else total + part
                begin += count
            sum_refs[index][:, columns] = total.astype(jnp.bfloat16)


def forward(rows_own, rows_other, slabs, vector=None):
    packed = vector is None
    counts = tuple(slab.shape[0] for slab in slabs)
    units = sum(counts)
    count, width = rows_own.shape
    vmem = pl.BlockSpec(memory_space=pltpu.VMEM)
    sums = jax.ShapeDtypeStruct((count, width), jnp.bfloat16)
    sigmas = jax.ShapeDtypeStruct((count, units), jnp.float32)
    outs = (sums, sums) + ((sigmas, sigmas) if packed else ())
    args = (rows_own, rows_other, *slabs) + (() if packed else (vector,))
    return pl.pallas_call(
        lambda *refs: forward_kernel(counts, packed, *refs),
        out_shape=outs,
        in_specs=[vmem] * len(args),
        out_specs=(vmem,) * len(outs),
        scratch_shapes=[pltpu.VMEM((count, units), jnp.bfloat16)] * 2,
        compiler_params=pltpu.CompilerParams(vmem_limit_bytes=40 * 2**20),
        cost_estimate=pl.CostEstimate(
            flops=8 * count * width * units,
            bytes_accessed=2 * width * (4 * count + units),
            transcendentals=2 * count * units,
        ),
    )(*args)


def body(
    samples,
    dual_weight,
    dual_vector,
    map_weight,
    map_vector,
    moment_weight,
    square_weight,
    moment_vector,
    square_vector,
):
    core = lax.axis_index("core")
    place = lax.axis_index("z")
    count, width = samples.shape
    inverse_rows = 1.0 / 6144

    packed = jnp.concatenate(
        [
            map_weight.astype(jnp.bfloat16),
            jnp.pad(map_vector.astype(jnp.bfloat16).T, ((0, 0), (0, extra - 2))),
        ],
        axis=1,
    )
    first = spread(spread(packed[:16], shift_x), shift_y)
    second = spread(spread(packed[16:], shift_y), shift_x)
    slab = jnp.concatenate([first, second], axis=0)
    weight = slab[:, :width]
    readout = slab[:, width].astype(jnp.float32)
    offset = slab[:, width + 1].astype(jnp.float32)

    rows_all = lax.all_gather(samples, "z", axis=0, tiled=True)
    rows_own = lax.dynamic_slice_in_dim(
        jnp.concatenate([rows_all, rows_all], axis=0), (place + 6) % 8 * count, 8 * count, axis=0
    )
    rows_other = other_core(rows_own)
    cut = 5 * count
    groups = [(rows_own[:cut], rows_other[:cut]), (rows_own[cut:], rows_other[cut:])]

    half = dual_weight.shape[0] // 2
    dual_half = lax.dynamic_slice_in_dim(dual_weight, core * half, half, axis=0)
    dual_small = lax.dynamic_slice_in_dim(dual_vector, core * half, half, axis=1)
    dual_small_received = lax.ppermute(dual_small, "xl", flip)
    dual_small_received, slab = lax.optimization_barrier((dual_small_received, slab))
    part = half // 4
    swap = [
        lax.ppermute(dual_half[part * i : part * (i + 1)], "xl", flip) for i in range(4)
    ]
    dual_pair = jnp.concatenate([dual_small, dual_small_received], axis=1)

    sum_own, sum_other, sigma_own, sigma_other = forward(rows_own, rows_other, [slab])
    sigma_near = (sigma_own[:cut], sigma_other[:cut])
    sigma_far = (sigma_own[cut:], sigma_other[cut:])

    def scaled_of(sigma):
        return (readout * sigma).astype(jnp.bfloat16)

    scaled_far, scaled_near = tuple(map(scaled_of, sigma_far)), tuple(map(scaled_of, sigma_near))

    def both_cores(own, other):
        return own.astype(jnp.float32) + other_core(other).astype(jnp.float32)

    sample_float = samples.astype(jnp.float32)
    far_sum = both_cores(sum_own[cut:], sum_other[cut:])
    near_sum = both_cores(sum_own[:cut], sum_other[:cut])
    far_sum, swap[0] = lax.optimization_barrier((far_sum, swap[0]))
    reduced, swap[1] = reduce_z(near_sum, far_sum, swap[1])
    mapped = sample_float + reduced
    mapped, swap[2] = lax.optimization_barrier((mapped, swap[2]))
    low_near, low_far, swap[3] = gather_z(mapped.astype(jnp.bfloat16), swap[3])
    dual_slabs = [dual_half, jnp.concatenate(swap, axis=0)]

    def dual_sum(low):
        return forward(low, other_core(low), dual_slabs, dual_pair)

    dual_near = dual_sum(low_near)
    dual_near, low_far = lax.optimization_barrier((dual_near, low_far))
    dual_far = dual_sum(low_far)
    dual_far = both_cores(*dual_far)
    dual_reduced, _ = reduce_z(both_cores(*dual_near), dual_far)
    dual_grad = mapped + dual_reduced
    residual = (sample_float - dual_grad).astype(jnp.bfloat16)
    residual_near, residual_far, _ = gather_z(residual)

    def curve_of(sigma, rows):
        pulled = contract_last(rows, weight)
        curve = readout * (sigma * (1.0 - sigma)) * pulled
        sums = jnp.stack([jnp.sum(sigma * pulled, axis=0), jnp.sum(curve, axis=0)], axis=1)
        return curve.astype(jnp.bfloat16), sums

    lefts, rights, small = [], [], 0.0
    for sigmas, scaleds, rows, pulled_own in (
        (sigma_near, scaled_near, groups[0], residual_near),
        (sigma_far, scaled_far, groups[1], residual_far),
    ):
        pulled_rows = (pulled_own, other_core(pulled_own))
        for i in range(2):
            curve, sums = curve_of(sigmas[i], pulled_rows[i])
            lefts += [scaleds[i], curve]
            rights += [pulled_rows[i], rows[i]]
            small = small + sums
    left_stack = jnp.concatenate(lefts, axis=0)
    right_stack = jnp.concatenate(rights, axis=0)
    grad_small = jnp.pad(
        (small * inverse_rows).astype(jnp.bfloat16), ((0, 0), (0, extra - 2))
    )

    def grad_part(begin, end):
        part = contract_first(left_stack[:, begin:end], right_stack) * inverse_rows
        return jnp.concatenate([part.astype(jnp.bfloat16), grad_small[begin:end]], axis=1)

    units = left_stack.shape[1]
    grad_first = collect(
        collect(grad_part(0, units // 2), shift_y).astype(jnp.bfloat16), shift_x
    )
    grad_second = collect(
        collect(grad_part(units // 2, units), shift_x).astype(jnp.bfloat16), shift_y
    )
    owner = jnp.concatenate([grad_first, grad_second], axis=0)
    owner_weight = owner[:, :width]
    owner_vector = owner[:, width : width + 2].T

    next_weight, next_moment_weight, next_square_weight = adam_update(
        map_weight, owner_weight, moment_weight, square_weight
    )
    raw_vector, next_moment_vector, next_square_vector = adam_update(
        map_vector, owner_vector, moment_vector, square_vector
    )
    next_vector = jnp.concatenate([jnp.maximum(raw_vector[0:1], 0.0), raw_vector[1:2]], axis=0)
    return (
        next_weight,
        next_vector,
        next_moment_weight,
        next_square_weight,
        next_moment_vector,
        next_square_vector,
    )


def solution(mesh):
    fsdp = ("xl", "z")
    rep = ("y", "xh", "core")
    fine = Mesh(mesh.devices.reshape(2, 8, 4, 2, 2), fsdp + rep)
    rows = P(fsdp + rep, None)
    columns = P(None, fsdp + rep)
    return jax.shard_map(
        body,
        mesh=fine,
        in_specs=(rows, P(fsdp, None), P(None, fsdp), rows, columns, rows, rows, columns, columns),
        out_specs=(rows, columns, rows, rows, columns, columns),
        check_vma=False,
    )
```

```python
import jax
import jax.numpy as jnp
from jax import lax
from jax.experimental import pallas as pl
from jax.experimental.pallas import tpu as pltpu
from jax.sharding import Mesh, PartitionSpec as P

beta_one = 0.9
beta_two = 0.999
learn_rate = 0.001
epsilon = 1e-08
adam_step = 10
extra = 128

flip = [(0, 1), (1, 0)]


def contract_last(left, right):
    return lax.dot_general(
        left, right, (((1,), (1,)), ((), ())), preferred_element_type=jnp.float32
    )


def contract_first(left, right):
    return lax.dot_general(
        left, right, (((0,), (0,)), ((), ())), preferred_element_type=jnp.float32
    )


def dot(left, right):
    return jnp.dot(left, right, preferred_element_type=jnp.float32)


def adam_update(param, grad, moment, square):
    moment_new = beta_one * moment + (1.0 - beta_one) * grad
    square_new = beta_two * square + (1.0 - beta_two) * grad * grad
    fix_one = 1.0 - beta_one**adam_step
    fix_two = 1.0 - beta_two**adam_step
    update = learn_rate * (moment_new / fix_one) / (jnp.sqrt(square_new / fix_two) + epsilon)
    return (param - update, moment_new, square_new)


def shift_y(value, step):
    return lax.ppermute(value, "y", [(i, (i + step) % 4) for i in range(4)])


ring_x = (0, 2, 1, 3)


def shift_x(value, step):
    return lax.ppermute(
        value, ("xl", "xh"), [(ring_x[i], ring_x[(i + step) % 4]) for i in range(4)]
    )


def spread_direct(value, shift):
    return jnp.concatenate([value] + [shift(value, step) for step in (1, 2, 3)], axis=0)


def collect_direct(value, shift):
    rows = value.shape[0] // 4
    low = value.astype(jnp.bfloat16)
    total = value[:rows]
    for step in (1, 2, 3):
        total = total + shift(low[rows * step : rows * (step + 1)], -step).astype(jnp.float32)
    return total


def spread(parts, shifts, ride):
    half = parts[0].shape[0] // 2
    sent = [shift(value, step) for value, shift in zip(parts, shifts) for step in (1, -1)]
    sent, ride = lax.optimization_barrier((sent, ride))
    again = []
    for index, shift in enumerate(shifts):
        again += [shift(sent[2 * index][:half], 1), shift(sent[2 * index + 1][half:], -1)]
    pieces = []
    for i, value in enumerate(parts):
        pieces += [value, sent[2 * i], again[2 * i], again[2 * i + 1], sent[2 * i + 1]]
    return pieces, ride


def collect(parts, shifts):
    wide, low = jnp.float32, jnp.bfloat16
    sent = []
    for (_, _, front, back, _), shift in zip(parts, shifts):
        sent += [shift(front, -1), shift(back, 1)]
    sent = lax.optimization_barrier(sent)
    half = sent[0].shape[0]
    final = []
    for index, ((_, behind, _, _, ahead), shift) in enumerate(zip(parts, shifts)):
        front, back = sent[2 * index].astype(wide), sent[2 * index + 1].astype(wide)
        behind = jnp.concatenate([(behind[:half].astype(wide) + front).astype(low), behind[half:]])
        ahead = jnp.concatenate([ahead[:half], (ahead[half:].astype(wide) + back).astype(low)])
        final += [shift(behind, -1), shift(ahead, 1)]
    final = lax.optimization_barrier(final)
    return [
        own[0].astype(wide) + final[2 * i].astype(wide) + final[2 * i + 1].astype(wide)
        for i, own in enumerate(parts)
    ]


def other_core(value):
    return lax.ppermute(value, "core", flip)


def shift_z(value, step):
    return lax.ppermute(value, "z", [(i, (i + step) % 8) for i in range(8)])


def gather_z(value, ride=None):
    middle = value.shape[1] // 2
    from_ahead, from_behind = shift_z(value, -2), shift_z(value, 2)
    next_ahead, next_behind = shift_z(value, -1), shift_z(value, 1)
    if ride is not None:
        from_behind, ride = lax.optimization_barrier((from_behind, ride))
    left, right = shift_z(from_behind[:, :middle], 2), shift_z(from_ahead[:, middle:], -2)
    third_ahead, third_behind = shift_z(from_ahead, -1), shift_z(from_behind, 1)
    return (
        jnp.concatenate([from_behind, next_behind, value, next_ahead, from_ahead], axis=0),
        jnp.concatenate(
            [third_ahead, jnp.concatenate([left, right], axis=1), third_behind], axis=0
        ),
        ride,
    )


def reduce_z(near_sum, far_sum, ride=None):
    wide = jnp.float32
    count = near_sum.shape[0] // 5
    middle = near_sum.shape[1] // 2

    def near_block(index):
        return near_sum[count * (index + 2) : count * (index + 3)]

    third_ahead, fourth, third_behind = (far_sum[count * i : count * (i + 1)] for i in range(3))
    low = jnp.bfloat16
    left = shift_z(fourth[:, :middle].astype(low), 2)
    right = shift_z(fourth[:, middle:].astype(low), -2)
    ahead = shift_z(third_ahead.astype(low), 1)
    behind = shift_z(third_behind.astype(low), -1)
    if ride is not None:
        left, ride = lax.optimization_barrier((left, ride))
    beside_ahead = shift_z(near_block(1).astype(low), 1)
    beside_behind = shift_z(near_block(-1).astype(low), -1)
    ahead_sum = near_block(2).astype(wide) + ahead.astype(wide)
    behind_sum = near_block(-2).astype(wide) + behind.astype(wide)
    ahead_sum = jnp.concatenate(
        [ahead_sum[:, :middle] + left.astype(wide), ahead_sum[:, middle:]], axis=1
    )
    behind_sum = jnp.concatenate(
        [behind_sum[:, :middle], behind_sum[:, middle:] + right.astype(wide)], axis=1
    )
    from_behind = shift_z(ahead_sum.astype(low), 2)
    from_ahead = shift_z(behind_sum.astype(low), -2)
    total = near_block(0).astype(wide) + beside_ahead.astype(wide) + beside_behind.astype(wide)
    return total + from_behind.astype(wide) + from_ahead.astype(wide), ride


tile = 512


def forward_kernel(counts, packed, *refs):
    own_ref, other_ref = refs[:2]
    slabs = refs[2 : 2 + len(counts)]
    refs = refs[2 + len(counts) :]
    if packed:
        slab, begin = refs[4], 0
        for piece, count in zip(slabs, counts):
            slab[begin : begin + count] = piece[...]
            begin += count
        slabs, counts = [slab], [begin]
        tail = slab[:, own_ref.shape[1] :]
        vector = contract_last(pick_rows(), tail)
        readout, offset = vector[0:1], vector[1:2]
        sum_refs, sigma_refs = refs[0:2], refs[2:4]
        scratch = refs[5:]
    else:
        readout, offset = refs[0][0:1], refs[0][1:2]
        sum_refs, sigma_refs = refs[1:3], None
        scratch = refs[3:]
    width = own_ref.shape[1]
    for index, rows in enumerate((own_ref, other_ref)):
        begin = 0
        for slab, count in zip(slabs, counts):
            for low in range(0, count, 256):
                size = min(256, count - low)
                hidden = contract_last(rows[...], slab[low : low + size, :width])
                span = slice(begin + low, begin + low + size)
                sigma = jax.nn.sigmoid(hidden + offset[:, span])
                if sigma_refs is not None:
                    sigma_refs[index][:, span] = sigma
                scratch[index][:, span] = (readout[:, span] * sigma).astype(jnp.bfloat16)
            begin += count

    @pl.loop(0, width // tile)
    def _(step):
        columns = pl.ds(pl.multiple_of(step * tile, tile), tile)
        for index in (1, 0):
            total, begin = None, 0
            for slab, count in zip(slabs, counts):
                part = dot(scratch[index][:, begin : begin + count], slab[:, columns])
                total = part if total is None else total + part
                begin += count
            sum_refs[index][:, columns] = total.astype(jnp.bfloat16)


def pick_rows():
    lane = lax.broadcasted_iota(jnp.int32, (8, extra), 1)
    row = lax.broadcasted_iota(jnp.int32, (8, extra), 0)
    return jnp.where(lane == row, 1.0, 0.0).astype(jnp.bfloat16)


def backward_kernel(scale, *refs):
    near_refs, far_refs = refs[0:2], refs[2:4]
    rows_refs, sigma_refs, slab = refs[4:6], refs[6:8], refs[8]
    out_refs, scratch = refs[9:-6], refs[-6:]
    width = rows_refs[0].shape[1]
    cut = near_refs[0].shape[0]
    readout = contract_last(pick_rows(), slab[:, width:])[0:1]
    sums = []
    for index in range(2):
        sigma_sum, curve_sum = 0.0, 0.0
        near_scaled, far_scaled, curves = scratch[3 * index : 3 * index + 3]
        for low in range(0, slab.shape[0], 256):
            span = slice(low, low + 256)
            factor = readout[:, span]
            near = contract_last(near_refs[index][...], slab[span, :width])
            far = contract_last(far_refs[index][...], slab[span, :width])
            pulled = jnp.concatenate([near, far], axis=0)
            sigma = sigma_refs[index][:, span]
            scaled = factor * sigma
            curve = scaled * (1.0 - sigma) * pulled
            near_scaled[span, :] = jnp.transpose(scaled[:cut]).astype(jnp.bfloat16)
            far_scaled[span, :] = jnp.transpose(scaled[cut:]).astype(jnp.bfloat16)
            curves[span, :] = jnp.transpose(curve).astype(jnp.bfloat16)
            pair = (jnp.sum(sigma * pulled, axis=0), jnp.sum(curve, axis=0))
            if index == 0:
                sums.append(pair)
            else:
                old = sums[low // 256]
                sums[low // 256] = (old[0] + pair[0], old[1] + pair[1])
    lefts = scratch
    rights = (near_refs[0], far_refs[0], rows_refs[0], near_refs[1], far_refs[1], rows_refs[1])

    def store(total, columns):
        begin = 0
        for ref in out_refs:
            ref[:, columns] = total[begin : begin + ref.shape[0]].astype(jnp.bfloat16)
            begin += ref.shape[0]

    @pl.loop(0, width // tile)
    def _(step):
        columns = pl.ds(pl.multiple_of(step * tile, tile), tile)
        total = None
        for left, right in zip(lefts, rights):
            part = dot(left[...], right[:, columns])
            total = part if total is None else total + part
        store(total * scale, columns)

    row = lax.broadcasted_iota(jnp.int32, (8, 256), 0)
    small = [jnp.where(row == 0, a[None], jnp.where(row == 1, b[None], 0.0)) for a, b in sums]
    small = (jnp.concatenate(small, axis=1) * scale).astype(jnp.bfloat16)
    store(contract_first(small, pick_rows()), slice(width, width + extra))


def backward(residuals, others, slab, scale):
    units, wide = slab.shape
    width = wide - extra
    near, far = residuals[0].shape[0], residuals[2].shape[0]
    count = near + far
    quarter = units // 8
    sizes = (quarter, quarter, quarter // 2, quarter // 2, quarter) * 2
    vmem = pl.BlockSpec(memory_space=pltpu.VMEM)
    args = (*residuals, *others, slab)
    return pl.pallas_call(
        lambda *refs: backward_kernel(scale, *refs),
        out_shape=tuple(jax.ShapeDtypeStruct((size, wide), jnp.bfloat16) for size in sizes),
        in_specs=[vmem] * len(args),
        out_specs=(vmem,) * len(sizes),
        scratch_shapes=[pltpu.VMEM((units, size), jnp.bfloat16) for size in (near, far, count)] * 2,
        compiler_params=pltpu.CompilerParams(vmem_limit_bytes=48 * 2**20),
        cost_estimate=pl.CostEstimate(
            flops=12 * count * width * units,
            bytes_accessed=2 * width * (4 * count + 2 * units),
            transcendentals=0,
        ),
    )(*args)


def forward(rows_own, rows_other, slabs, vector=None):
    packed = vector is None
    counts = tuple(slab.shape[0] for slab in slabs)
    units = sum(counts)
    count, width = rows_own.shape
    vmem = pl.BlockSpec(memory_space=pltpu.VMEM)
    sums = jax.ShapeDtypeStruct((count, width), jnp.bfloat16)
    sigmas = jax.ShapeDtypeStruct((count, units), jnp.float32)
    outs = (sums, sums)
    if packed:
        outs += (sigmas, sigmas, jax.ShapeDtypeStruct((units, slabs[0].shape[1]), jnp.bfloat16))
    args = (rows_own, rows_other, *slabs) + (() if packed else (vector,))
    return pl.pallas_call(
        lambda *refs: forward_kernel(counts, packed, *refs),
        out_shape=outs,
        in_specs=[vmem] * len(args),
        out_specs=(vmem,) * len(outs),
        scratch_shapes=[pltpu.VMEM((count, units), jnp.bfloat16)] * 2,
        compiler_params=pltpu.CompilerParams(vmem_limit_bytes=40 * 2**20),
        cost_estimate=pl.CostEstimate(
            flops=8 * count * width * units,
            bytes_accessed=2 * width * (4 * count + units),
            transcendentals=2 * count * units,
        ),
    )(*args)


def body(
    samples,
    dual_weight,
    dual_vector,
    map_weight,
    map_vector,
    moment_weight,
    square_weight,
    moment_vector,
    square_vector,
):
    core = lax.axis_index("core")
    place = lax.axis_index("z")
    count, width = samples.shape
    inverse_rows = 1.0 / 6144

    packed = jnp.concatenate(
        [
            map_weight.astype(jnp.bfloat16),
            jnp.pad(map_vector.astype(jnp.bfloat16).T, ((0, 0), (0, extra - 2))),
        ],
        axis=1,
    )
    rows_all = lax.all_gather(samples, "z", axis=0, tiled=True)
    halves = [spread_direct(packed[:16], shift_x), spread_direct(packed[16:], shift_y)]
    pieces, rows_all = spread(halves, [shift_y, shift_x], rows_all)
    rows_own = lax.dynamic_slice_in_dim(
        jnp.concatenate([rows_all, rows_all], axis=0), (place + 6) % 8 * count, 8 * count, axis=0
    )
    rows_other = other_core(rows_own)
    cut = 5 * count

    half = dual_weight.shape[0] // 2
    dual_half = lax.dynamic_slice_in_dim(dual_weight, core * half, half, axis=0)
    dual_small = lax.dynamic_slice_in_dim(dual_vector, core * half, half, axis=1)
    dual_small_received = lax.ppermute(dual_small, "xl", flip)
    dual_small_received, rows_own = lax.optimization_barrier((dual_small_received, rows_own))
    dual_pair = jnp.concatenate([dual_small, dual_small_received], axis=1)
    cuts = (0, 64, 160, half)
    swap = [lax.ppermute(dual_half[cuts[i] : cuts[i + 1]], "xl", flip) for i in range(3)]

    sum_own, sum_other, sigma_own, sigma_other, slab = forward(rows_own, rows_other, pieces)

    def both_cores(own, other):
        return own.astype(jnp.float32) + other_core(other).astype(jnp.float32)

    sample_float = samples.astype(jnp.float32)
    far_sum = both_cores(sum_own[cut:], sum_other[cut:])
    near_sum = both_cores(sum_own[:cut], sum_other[:cut])
    reduced, swap[0] = reduce_z(near_sum, far_sum, swap[0])
    mapped, swap[1] = lax.optimization_barrier((sample_float + reduced, swap[1]))
    low_near, low_far, swap[2] = gather_z(mapped.astype(jnp.bfloat16), swap[2])
    dual_slab = jnp.concatenate([dual_half, *swap], axis=0)

    def dual_sum(low):
        return forward(low, other_core(low), [dual_slab], dual_pair)

    dual_near = dual_sum(low_near)
    dual_near, low_far = lax.optimization_barrier((dual_near, low_far))
    dual_far = dual_sum(low_far)
    dual_far = both_cores(*dual_far)
    dual_reduced, _ = reduce_z(both_cores(*dual_near), dual_far)
    dual_grad = mapped + dual_reduced
    residual = (sample_float - dual_grad).astype(jnp.bfloat16)
    residual_near, residual_far, _ = gather_z(residual)

    grads = backward(
        [residual_near, other_core(residual_near), residual_far, other_core(residual_far)],
        [rows_own, rows_other, sigma_own, sigma_other],
        slab,
        inverse_rows,
    )
    across = collect([grads[:5], grads[5:]], [shift_y, shift_x])
    grad_first = collect_direct(across[0], shift_x)
    grad_second = collect_direct(across[1], shift_y)
    owner = jnp.concatenate([grad_first, grad_second], axis=0)
    owner_weight = owner[:, :width]
    owner_vector = owner[:, width : width + 2].T

    next_weight, next_moment_weight, next_square_weight = adam_update(
        map_weight, owner_weight, moment_weight, square_weight
    )
    raw_vector, next_moment_vector, next_square_vector = adam_update(
        map_vector, owner_vector, moment_vector, square_vector
    )
    next_vector = jnp.concatenate([jnp.maximum(raw_vector[0:1], 0.0), raw_vector[1:2]], axis=0)
    return (
        next_weight,
        next_vector,
        next_moment_weight,
        next_square_weight,
        next_moment_vector,
        next_square_vector,
    )


def solution(mesh):
    fsdp = ("xl", "z")
    rep = ("y", "xh", "core")
    fine = Mesh(mesh.devices.reshape(2, 8, 4, 2, 2), fsdp + rep)
    rows = P(fsdp + rep, None)
    columns = P(None, fsdp + rep)
    return jax.shard_map(
        body,
        mesh=fine,
        in_specs=(rows, P(fsdp, None), P(None, fsdp), rows, columns, rows, rows, columns, columns),
        out_specs=(rows, columns, rows, rows, columns, columns),
        check_vma=False,
    )
```

```python
import jax
import jax.numpy as jnp
from jax import lax
from jax.experimental import pallas as pl
from jax.experimental.pallas import tpu as pltpu
from jax.sharding import Mesh, PartitionSpec as P

beta_one = 0.9
beta_two = 0.999
learn_rate = 0.001
epsilon = 1e-08
adam_step = 10
extra = 128

flip = [(0, 1), (1, 0)]


def contract_last(left, right):
    return lax.dot_general(
        left, right, (((1,), (1,)), ((), ())), preferred_element_type=jnp.float32
    )


def contract_first(left, right):
    return lax.dot_general(
        left, right, (((0,), (0,)), ((), ())), preferred_element_type=jnp.float32
    )


def dot(left, right):
    return jnp.dot(left, right, preferred_element_type=jnp.float32)


def adam_update(param, grad, moment, square):
    moment_new = beta_one * moment + (1.0 - beta_one) * grad
    square_new = beta_two * square + (1.0 - beta_two) * grad * grad
    fix_one = 1.0 - beta_one**adam_step
    fix_two = 1.0 - beta_two**adam_step
    update = learn_rate * (moment_new / fix_one) / (jnp.sqrt(square_new / fix_two) + epsilon)
    return (param - update, moment_new, square_new)


def shift_y(value, step):
    return lax.ppermute(value, "y", [(i, (i + step) % 4) for i in range(4)])


ring_x = (0, 2, 1, 3)


def shift_x(value, step):
    return lax.ppermute(
        value, ("xl", "xh"), [(ring_x[i], ring_x[(i + step) % 4]) for i in range(4)]
    )


def spread_direct(value, shift):
    return jnp.concatenate([value] + [shift(value, step) for step in (1, 2, 3)], axis=0)


def collect_direct(value, shift):
    rows = value.shape[0] // 4
    low = value.astype(jnp.bfloat16)
    total = value[:rows]
    for step in (1, 2, 3):
        total = total + shift(low[rows * step : rows * (step + 1)], -step).astype(jnp.float32)
    return total


def spread(parts, shifts, ride):
    half = parts[0].shape[0] // 2
    sent = [shift(value, step) for value, shift in zip(parts, shifts) for step in (1, -1)]
    sent = lax.optimization_barrier(sent)
    again = [shifts[0](sent[0][:half], 1), shifts[0](sent[1][half:], -1)]
    sent[2:], ride = lax.optimization_barrier((sent[2:], ride))
    again += [shifts[1](sent[2][:half], 1), shifts[1](sent[3][half:], -1)]
    pieces = []
    for i, value in enumerate(parts):
        pieces += [value, sent[2 * i], again[2 * i], again[2 * i + 1], sent[2 * i + 1]]
    return pieces, ride


def collect(parts, shifts):
    wide, low = jnp.float32, jnp.bfloat16
    sent = []
    for (_, _, front, back, _), shift in zip(parts, shifts):
        sent += [shift(front, -1), shift(back, 1)]
    sent = lax.optimization_barrier(sent)
    half = sent[0].shape[0]
    final = []
    for index, ((_, behind, _, _, ahead), shift) in enumerate(zip(parts, shifts)):
        front, back = sent[2 * index].astype(wide), sent[2 * index + 1].astype(wide)
        behind = jnp.concatenate([(behind[:half].astype(wide) + front).astype(low), behind[half:]])
        ahead = jnp.concatenate([ahead[:half], (ahead[half:].astype(wide) + back).astype(low)])
        final += [shift(behind, -1), shift(ahead, 1)]
    final = lax.optimization_barrier(final)
    return [
        own[0].astype(wide) + final[2 * i].astype(wide) + final[2 * i + 1].astype(wide)
        for i, own in enumerate(parts)
    ]


def other_core(value):
    return lax.ppermute(value, "core", flip)


def shift_z(value, step):
    return lax.ppermute(value, "z", [(i, (i + step) % 8) for i in range(8)])


def gather_z(value):
    middle = value.shape[1] // 2
    from_ahead, from_behind = shift_z(value, -2), shift_z(value, 2)
    next_ahead, next_behind = shift_z(value, -1), shift_z(value, 1)
    left, right = shift_z(from_behind[:, :middle], 2), shift_z(from_ahead[:, middle:], -2)
    third_ahead, third_behind = shift_z(from_ahead, -1), shift_z(from_behind, 1)
    return (
        jnp.concatenate([from_behind, next_behind, value, next_ahead, from_ahead], axis=0),
        jnp.concatenate(
            [third_ahead, jnp.concatenate([left, right], axis=1), third_behind], axis=0
        ),
    )


def reduce_z(near_sum, far_sum):
    wide = jnp.float32
    count = near_sum.shape[0] // 5
    middle = near_sum.shape[1] // 2

    def near_block(index):
        return near_sum[count * (index + 2) : count * (index + 3)]

    third_ahead, fourth, third_behind = (far_sum[count * i : count * (i + 1)] for i in range(3))
    low = jnp.bfloat16
    left = shift_z(fourth[:, :middle].astype(low), 2)
    right = shift_z(fourth[:, middle:].astype(low), -2)
    ahead = shift_z(third_ahead.astype(low), 1)
    behind = shift_z(third_behind.astype(low), -1)
    beside_ahead = shift_z(near_block(1).astype(low), 1)
    beside_behind = shift_z(near_block(-1).astype(low), -1)
    ahead_sum = near_block(2).astype(wide) + ahead.astype(wide)
    behind_sum = near_block(-2).astype(wide) + behind.astype(wide)
    ahead_sum = jnp.concatenate(
        [ahead_sum[:, :middle] + left.astype(wide), ahead_sum[:, middle:]], axis=1
    )
    behind_sum = jnp.concatenate(
        [behind_sum[:, :middle], behind_sum[:, middle:] + right.astype(wide)], axis=1
    )
    from_behind = shift_z(ahead_sum.astype(low), 2)
    from_ahead = shift_z(behind_sum.astype(low), -2)
    total = near_block(0).astype(wide) + beside_ahead.astype(wide) + beside_behind.astype(wide)
    return total + from_behind.astype(wide) + from_ahead.astype(wide)


tile = 512


def forward_kernel(counts, packed, *refs):
    own_ref, other_ref = refs[:2]
    slabs = refs[2 : 2 + len(counts)]
    refs = refs[2 + len(counts) :]
    if packed:
        slab, begin, copies = refs[4], 0, []
        for index, (piece, count) in enumerate(zip(slabs, counts)):
            target = slab.at[begin : begin + count]
            copies.append(pltpu.make_async_copy(piece, target, refs[7].at[index]))
            begin += count
        for copy in copies:
            copy.start()
        for copy in copies:
            copy.wait()
        slabs, counts = [slab], [begin]
        tail = slab[:, own_ref.shape[1] :]
        vector = contract_last(pick_rows(), tail)
        readout, offset = vector[0:1], vector[1:2]
        sum_refs, sigma_refs = refs[0:2], refs[2:4]
        scratch = refs[5:7]
    else:
        readout, offset = refs[0][0:1], refs[0][1:2]
        sum_refs, sigma_refs = refs[1:3], None
        scratch = refs[3:]
    width = own_ref.shape[1]
    for index, rows in enumerate((own_ref, other_ref)):
        begin = 0
        for slab, count in zip(slabs, counts):
            for low in range(0, count, 256):
                size = min(256, count - low)
                hidden = contract_last(rows[...], slab[low : low + size, :width])
                span = slice(begin + low, begin + low + size)
                sigma = jax.nn.sigmoid(hidden + offset[:, span])
                if sigma_refs is not None:
                    sigma_refs[index][:, span] = sigma
                scratch[index][:, span] = (readout[:, span] * sigma).astype(jnp.bfloat16)
            begin += count

    @pl.loop(0, width // tile)
    def _(step):
        columns = pl.ds(pl.multiple_of(step * tile, tile), tile)
        for index in (1, 0):
            total, begin = None, 0
            for slab, count in zip(slabs, counts):
                part = dot(scratch[index][:, begin : begin + count], slab[:, columns])
                total = part if total is None else total + part
                begin += count
            sum_refs[index][:, columns] = total.astype(jnp.bfloat16)


def pick_rows():
    lane = lax.broadcasted_iota(jnp.int32, (8, extra), 1)
    row = lax.broadcasted_iota(jnp.int32, (8, extra), 0)
    return jnp.where(lane == row, 1.0, 0.0).astype(jnp.bfloat16)


def backward_kernel(scale, *refs):
    near_refs, far_refs = refs[0:2], refs[2:4]
    rows_refs, sigma_refs, slab = refs[4:6], refs[6:8], refs[8]
    out_refs, left, right = refs[9:-2], refs[-2], refs[-1]
    units = slab.shape[0]
    count, width = rows_refs[0].shape
    cut = near_refs[0].shape[0]
    readout = contract_last(pick_rows(), slab[:, width:])[0:1]
    none = jnp.bfloat16(0.0)
    starts = ((0, 512, 768), (256, 640, 896))
    for index in range(2):
        for begin, ref in zip(starts[index], (rows_refs[index], near_refs[index], far_refs[index])):
            size = ref.shape[0]
            room, whole = (256 if size > 128 else 128), size // 16 * 16
            right[begin + whole : begin + room] = jnp.full((room - whole, width), none)
            right[begin : begin + size] = ref[...]
            left[:, begin + room - 128 : begin + room] = jnp.full((units, 128), none)
    sums = []
    for index in range(2):
        for low in range(0, units, 256):
            span = slice(low, low + 256)
            factor = readout[:, span]
            near = contract_last(near_refs[index][...], slab[span, :width])
            far = contract_last(far_refs[index][...], slab[span, :width])
            pulled = jnp.concatenate([near, far], axis=0)
            sigma = sigma_refs[index][:, span]
            scaled = factor * sigma
            curve = scaled * (1.0 - sigma) * pulled
            parts = (curve, scaled[:cut], scaled[cut:])
            for begin, part in zip(starts[index], parts):
                left[span, begin : begin + part.shape[0]] = jnp.transpose(part).astype(jnp.bfloat16)
            pair = (jnp.sum(sigma * pulled, axis=0), jnp.sum(curve, axis=0))
            if index == 0:
                sums.append(pair)
            else:
                old = sums[low // 256]
                sums[low // 256] = (old[0] + pair[0], old[1] + pair[1])

    def store(total, columns):
        begin = 0
        for ref in out_refs:
            ref[:, columns] = total[begin : begin + ref.shape[0]].astype(jnp.bfloat16)
            begin += ref.shape[0]

    @pl.loop(0, width // tile)
    def _(step):
        columns = pl.ds(pl.multiple_of(step * tile, tile), tile)
        total = dot(left[...], right[:, columns])
        store(total * scale, columns)

    row = lax.broadcasted_iota(jnp.int32, (8, 256), 0)
    small = [jnp.where(row == 0, a[None], jnp.where(row == 1, b[None], 0.0)) for a, b in sums]
    small = (jnp.concatenate(small, axis=1) * scale).astype(jnp.bfloat16)
    store(contract_first(small, pick_rows()), slice(width, width + extra))


def backward(residuals, others, slab, scale):
    units, wide = slab.shape
    width = wide - extra
    near, far = residuals[0].shape[0], residuals[2].shape[0]
    count = near + far
    quarter = units // 8
    sizes = (quarter, quarter, quarter // 2, quarter // 2, quarter) * 2
    vmem = pl.BlockSpec(memory_space=pltpu.VMEM)
    args = (*residuals, *others, slab)
    return pl.pallas_call(
        lambda *refs: backward_kernel(scale, *refs),
        out_shape=tuple(jax.ShapeDtypeStruct((size, wide), jnp.bfloat16) for size in sizes),
        in_specs=[vmem] * len(args),
        out_specs=(vmem,) * len(sizes),
        scratch_shapes=[pltpu.VMEM((units, 1024), jnp.bfloat16), pltpu.VMEM((1024, width), jnp.bfloat16)],
        compiler_params=pltpu.CompilerParams(vmem_limit_bytes=48 * 2**20),
        cost_estimate=pl.CostEstimate(
            flops=12 * count * width * units,
            bytes_accessed=2 * width * (4 * count + 2 * units),
            transcendentals=0,
        ),
    )(*args)


def forward(rows_own, rows_other, slabs, vector=None):
    packed = vector is None
    counts = tuple(slab.shape[0] for slab in slabs)
    units = sum(counts)
    count, width = rows_own.shape
    vmem = pl.BlockSpec(memory_space=pltpu.VMEM)
    sums = jax.ShapeDtypeStruct((count, width), jnp.bfloat16)
    sigmas = jax.ShapeDtypeStruct((count, units), jnp.float32)
    outs = (sums, sums)
    if packed:
        outs += (sigmas, sigmas, jax.ShapeDtypeStruct((units, slabs[0].shape[1]), jnp.bfloat16))
    args = (rows_own, rows_other, *slabs) + (() if packed else (vector,))
    return pl.pallas_call(
        lambda *refs: forward_kernel(counts, packed, *refs),
        out_shape=outs,
        in_specs=[vmem] * 2 + [pl.BlockSpec(memory_space=pl.ANY) if packed else vmem] * (len(args) - 2),
        out_specs=(vmem,) * len(outs),
        scratch_shapes=[pltpu.VMEM((count, units), jnp.bfloat16)] * 2
        + ([pltpu.SemaphoreType.DMA((len(slabs),))] if packed else []),
        compiler_params=pltpu.CompilerParams(vmem_limit_bytes=40 * 2**20),
        cost_estimate=pl.CostEstimate(
            flops=8 * count * width * units,
            bytes_accessed=2 * width * (4 * count + units),
            transcendentals=2 * count * units,
        ),
    )(*args)


def body(
    samples,
    dual_weight,
    dual_vector,
    map_weight,
    map_vector,
    moment_weight,
    square_weight,
    moment_vector,
    square_vector,
):
    core = lax.axis_index("core")
    place = lax.axis_index("z")
    count, width = samples.shape
    inverse_rows = 1.0 / 6144

    packed = jnp.concatenate(
        [
            map_weight.astype(jnp.bfloat16),
            jnp.pad(map_vector.astype(jnp.bfloat16).T, ((0, 0), (0, extra - 2))),
        ],
        axis=1,
    )
    rows_all = lax.all_gather(samples, "z", axis=0, tiled=True)
    half = dual_weight.shape[0] // 2
    dual_half = lax.dynamic_slice_in_dim(dual_weight, core * half, half, axis=0)
    swap = [
        lax.ppermute(dual_half[: half // 2], "xl", flip),
        lax.ppermute(dual_half[half // 2 :], "xl", flip),
    ]
    halves = [spread_direct(packed[:16], shift_x), spread_direct(packed[16:], shift_y)]
    pieces, (rows_all, swap[0]) = spread(halves, [shift_y, shift_x], (rows_all, swap[0]))
    rows_own = lax.dynamic_slice_in_dim(
        jnp.concatenate([rows_all, rows_all], axis=0), (place + 6) % 8 * count, 8 * count, axis=0
    )
    rows_other = other_core(rows_own)
    cut = 5 * count

    dual_small = lax.dynamic_slice_in_dim(dual_vector, core * half, half, axis=1)
    dual_small_received = lax.ppermute(dual_small, "xl", flip)
    dual_small_received, rows_own = lax.optimization_barrier((dual_small_received, rows_own))
    dual_pair = jnp.concatenate([dual_small, dual_small_received], axis=1)
    sum_own, sum_other, sigma_own, sigma_other, slab = forward(rows_own, rows_other, pieces)

    def both_cores(own, other):
        return own.astype(jnp.float32) + other_core(other).astype(jnp.float32)

    sample_float = samples.astype(jnp.float32)
    far_sum = both_cores(sum_own[cut:], sum_other[cut:])
    near_sum = both_cores(sum_own[:cut], sum_other[:cut])
    mapped = sample_float + reduce_z(near_sum, far_sum)
    low_near, low_far = gather_z(mapped.astype(jnp.bfloat16))
    dual_slabs = [dual_half, *swap]

    def dual_sum(low):
        return forward(low, other_core(low), dual_slabs, dual_pair)

    dual_near = dual_sum(low_near)
    dual_near, low_far = lax.optimization_barrier((dual_near, low_far))
    dual_far = dual_sum(low_far)
    dual_far = both_cores(*dual_far)
    dual_grad = mapped + reduce_z(both_cores(*dual_near), dual_far)
    residual = (sample_float - dual_grad).astype(jnp.bfloat16)
    residual_near, residual_far = gather_z(residual)

    grads = backward(
        [residual_near, other_core(residual_near), residual_far, other_core(residual_far)],
        [rows_own, rows_other, sigma_own, sigma_other],
        slab,
        inverse_rows,
    )
    across = collect([grads[:5], grads[5:]], [shift_y, shift_x])
    grad_first = collect_direct(across[0], shift_x)
    grad_second = collect_direct(across[1], shift_y)
    owner = jnp.concatenate([grad_first, grad_second], axis=0)
    owner_weight = owner[:, :width]
    owner_vector = owner[:, width : width + 2].T

    next_weight, next_moment_weight, next_square_weight = adam_update(
        map_weight, owner_weight, moment_weight, square_weight
    )
    raw_vector, next_moment_vector, next_square_vector = adam_update(
        map_vector, owner_vector, moment_vector, square_vector
    )
    next_vector = jnp.concatenate([jnp.maximum(raw_vector[0:1], 0.0), raw_vector[1:2]], axis=0)
    return (
        next_weight,
        next_vector,
        next_moment_weight,
        next_square_weight,
        next_moment_vector,
        next_square_vector,
    )


def solution(mesh):
    fsdp = ("xl", "z")
    rep = ("y", "xh", "core")
    fine = Mesh(mesh.devices.reshape(2, 8, 4, 2, 2), fsdp + rep)
    rows = P(fsdp + rep, None)
    columns = P(None, fsdp + rep)
    return jax.shard_map(
        body,
        mesh=fine,
        in_specs=(rows, P(fsdp, None), P(None, fsdp), rows, columns, rows, rows, columns, columns),
        out_specs=(rows, columns, rows, rows, columns, columns),
        check_vma=False,
    )
```

```python
import jax
import jax.numpy as jnp
from jax import lax
from jax.experimental import pallas as pl
from jax.experimental.pallas import tpu as pltpu
from jax.sharding import Mesh, PartitionSpec as P

beta_one = 0.9
beta_two = 0.999
learn_rate = 0.001
epsilon = 1e-08
adam_step = 10
extra = 128

flip = [(0, 1), (1, 0)]


def contract_last(left, right):
    return lax.dot_general(
        left, right, (((1,), (1,)), ((), ())), preferred_element_type=jnp.float32
    )


def contract_first(left, right):
    return lax.dot_general(
        left, right, (((0,), (0,)), ((), ())), preferred_element_type=jnp.float32
    )


def dot(left, right):
    return jnp.dot(left, right, preferred_element_type=jnp.float32)


def adam_update(param, grad, moment, square):
    moment_new = beta_one * moment + (1.0 - beta_one) * grad
    square_new = beta_two * square + (1.0 - beta_two) * grad * grad
    fix_one = 1.0 - beta_one**adam_step
    fix_two = 1.0 - beta_two**adam_step
    update = learn_rate * (moment_new / fix_one) / (jnp.sqrt(square_new / fix_two) + epsilon)
    return (param - update, moment_new, square_new)


def shift_y(value, step):
    return lax.ppermute(value, "y", [(i, (i + step) % 4) for i in range(4)])


ring_x = (0, 2, 1, 3)


def shift_x(value, step):
    return lax.ppermute(
        value, ("xl", "xh"), [(ring_x[i], ring_x[(i + step) % 4]) for i in range(4)]
    )


def spread_direct(value, shift):
    return jnp.concatenate([value] + [shift(value, step) for step in (1, 2, 3)], axis=0)


def collect_direct(value, shift):
    rows = value.shape[0] // 4
    low = value.astype(jnp.bfloat16)
    total = value[:rows]
    for step in (1, 2, 3):
        total = total + shift(low[rows * step : rows * (step + 1)], -step).astype(jnp.float32)
    return total


def spread(parts, shifts, ride):
    half = parts[0].shape[0] // 2
    sent = [shift(value, step) for value, shift in zip(parts, shifts) for step in (1, -1)]
    sent = lax.optimization_barrier(sent)
    again = [shifts[0](sent[0][:half], 1), shifts[0](sent[1][half:], -1)]
    sent[2:], again, ride = lax.optimization_barrier((sent[2:], again, ride))
    again += [shifts[1](sent[2][:half], 1), shifts[1](sent[3][half:], -1)]
    pieces = []
    for i, value in enumerate(parts):
        pieces += [value, sent[2 * i], again[2 * i], again[2 * i + 1], sent[2 * i + 1]]
    return pieces, ride


def collect(parts, shifts):
    wide, low = jnp.float32, jnp.bfloat16
    sent = []
    for (_, _, front, back, _), shift in zip(parts, shifts):
        sent += [shift(front, -1), shift(back, 1)]
    sent = lax.optimization_barrier(sent)
    half = sent[0].shape[0]
    final = []
    for index, ((_, behind, _, _, ahead), shift) in enumerate(zip(parts, shifts)):
        front, back = sent[2 * index].astype(wide), sent[2 * index + 1].astype(wide)
        behind = jnp.concatenate([(behind[:half].astype(wide) + front).astype(low), behind[half:]])
        ahead = jnp.concatenate([ahead[:half], (ahead[half:].astype(wide) + back).astype(low)])
        final += [shift(behind, -1), shift(ahead, 1)]
    final = lax.optimization_barrier(final)
    return [
        own[0].astype(wide) + final[2 * i].astype(wide) + final[2 * i + 1].astype(wide)
        for i, own in enumerate(parts)
    ]


def other_core(value):
    return lax.ppermute(value, "core", flip)


def shift_z(value, step):
    return lax.ppermute(value, "z", [(i, (i + step) % 8) for i in range(8)])


def gather_z(value):
    middle = value.shape[1] // 2
    from_ahead, from_behind = shift_z(value, -2), shift_z(value, 2)
    next_ahead, next_behind = shift_z(value, -1), shift_z(value, 1)
    left, right = shift_z(from_behind[:, :middle], 2), shift_z(from_ahead[:, middle:], -2)
    third_ahead, third_behind = shift_z(from_ahead, -1), shift_z(from_behind, 1)
    return (
        jnp.concatenate([from_behind, next_behind, value, next_ahead, from_ahead], axis=0),
        jnp.concatenate(
            [third_ahead, jnp.concatenate([left, right], axis=1), third_behind], axis=0
        ),
    )


def reduce_z(near_sum, far_sum):
    wide = jnp.float32
    count = near_sum.shape[0] // 5
    middle = near_sum.shape[1] // 2

    def near_block(index):
        return near_sum[count * (index + 2) : count * (index + 3)]

    third_ahead, fourth, third_behind = (far_sum[count * i : count * (i + 1)] for i in range(3))
    low = jnp.bfloat16
    left = shift_z(fourth[:, :middle].astype(low), 2)
    right = shift_z(fourth[:, middle:].astype(low), -2)
    ahead = shift_z(jnp.concatenate([third_ahead, near_block(1)], axis=0).astype(low), 1)
    behind = shift_z(jnp.concatenate([third_behind, near_block(-1)], axis=0).astype(low), -1)
    ahead, beside_ahead = ahead[:count], ahead[count:]
    behind, beside_behind = behind[:count], behind[count:]
    ahead_sum = near_block(2).astype(wide) + ahead.astype(wide)
    behind_sum = near_block(-2).astype(wide) + behind.astype(wide)
    ahead_sum = jnp.concatenate(
        [ahead_sum[:, :middle] + left.astype(wide), ahead_sum[:, middle:]], axis=1
    )
    behind_sum = jnp.concatenate(
        [behind_sum[:, :middle], behind_sum[:, middle:] + right.astype(wide)], axis=1
    )
    from_behind = shift_z(ahead_sum.astype(low), 2)
    from_ahead = shift_z(behind_sum.astype(low), -2)
    total = near_block(0).astype(wide) + beside_ahead.astype(wide) + beside_behind.astype(wide)
    return total + from_behind.astype(wide) + from_ahead.astype(wide)


tile = 512


def forward_kernel(counts, packed, *refs):
    own_ref, other_ref = refs[:2]
    slabs = refs[2 : 2 + len(counts)]
    refs = refs[2 + len(counts) :]
    if packed:
        slab, begin, copies = refs[4], 0, []
        for index, (piece, count) in enumerate(zip(slabs, counts)):
            target = slab.at[begin : begin + count]
            copies.append(pltpu.make_async_copy(piece, target, refs[7].at[index]))
            begin += count
        for copy in copies:
            copy.start()
        for copy in copies:
            copy.wait()
        slabs, counts = [slab], [begin]
        tail = slab[:, own_ref.shape[1] :]
        vector = contract_last(pick_rows(), tail)
        readout, offset = vector[0:1], vector[1:2]
        sum_refs, sigma_refs = refs[0:2], refs[2:4]
        scratch = refs[5:7]
    else:
        readout, offset = refs[0][0:1], refs[0][1:2]
        sum_refs, sigma_refs = refs[1:3], None
        scratch = refs[3:]
    width = own_ref.shape[1]
    for index, rows in enumerate((own_ref, other_ref)):
        begin = 0
        for slab, count in zip(slabs, counts):
            for low in range(0, count, 256):
                size = min(256, count - low)
                hidden = contract_last(rows[...], slab[low : low + size, :width])
                span = slice(begin + low, begin + low + size)
                sigma = jax.nn.sigmoid(hidden + offset[:, span])
                if sigma_refs is not None:
                    sigma_refs[index][:, span] = sigma
                scratch[index][:, span] = (readout[:, span] * sigma).astype(jnp.bfloat16)
            begin += count

    @pl.loop(0, width // tile)
    def _(step):
        columns = pl.ds(pl.multiple_of(step * tile, tile), tile)
        for index in (1, 0):
            total, begin = None, 0
            for slab, count in zip(slabs, counts):
                part = dot(scratch[index][:, begin : begin + count], slab[:, columns])
                total = part if total is None else total + part
                begin += count
            sum_refs[index][:, columns] = total.astype(jnp.bfloat16)


def pick_rows():
    lane = lax.broadcasted_iota(jnp.int32, (8, extra), 1)
    row = lax.broadcasted_iota(jnp.int32, (8, extra), 0)
    return jnp.where(lane == row, 1.0, 0.0).astype(jnp.bfloat16)


def backward_kernel(scale, *refs):
    near_refs, far_refs = refs[0:2], refs[2:4]
    rows_refs, sigma_refs, slab = refs[4:6], refs[6:8], refs[8]
    out_refs, left, right = refs[9:-2], refs[-2], refs[-1]
    units = slab.shape[0]
    count, width = rows_refs[0].shape
    cut = near_refs[0].shape[0]
    readout = contract_last(pick_rows(), slab[:, width:])[0:1]
    none = jnp.bfloat16(0.0)
    starts = ((0, 512, 768), (256, 640, 896))
    for index in range(2):
        for begin, ref in zip(starts[index], (rows_refs[index], near_refs[index], far_refs[index])):
            size = ref.shape[0]
            room, whole = (256 if size > 128 else 128), size // 16 * 16
            right[begin + whole : begin + room] = jnp.full((room - whole, width), none)
            right[begin : begin + size] = ref[...]
            left[:, begin + room - 128 : begin + room] = jnp.full((units, 128), none)
    sums = []
    for index in range(2):
        for low in range(0, units, 256):
            span = slice(low, low + 256)
            factor = readout[:, span]
            near = contract_last(near_refs[index][...], slab[span, :width])
            far = contract_last(far_refs[index][...], slab[span, :width])
            pulled = jnp.concatenate([near, far], axis=0)
            sigma = sigma_refs[index][:, span]
            scaled = factor * sigma
            curve = scaled * (1.0 - sigma) * pulled
            parts = (curve, scaled[:cut], scaled[cut:])
            for begin, part in zip(starts[index], parts):
                left[span, begin : begin + part.shape[0]] = jnp.transpose(part).astype(jnp.bfloat16)
            pair = (jnp.sum(sigma * pulled, axis=0), jnp.sum(curve, axis=0))
            if index == 0:
                sums.append(pair)
            else:
                old = sums[low // 256]
                sums[low // 256] = (old[0] + pair[0], old[1] + pair[1])

    def store(total, columns):
        begin = 0
        for ref in out_refs:
            ref[:, columns] = total[begin : begin + ref.shape[0]].astype(jnp.bfloat16)
            begin += ref.shape[0]

    @pl.loop(0, width // tile)
    def _(step):
        columns = pl.ds(pl.multiple_of(step * tile, tile), tile)
        total = dot(left[...], right[:, columns])
        store(total * scale, columns)

    row = lax.broadcasted_iota(jnp.int32, (8, 256), 0)
    small = [jnp.where(row == 0, a[None], jnp.where(row == 1, b[None], 0.0)) for a, b in sums]
    small = (jnp.concatenate(small, axis=1) * scale).astype(jnp.bfloat16)
    store(contract_first(small, pick_rows()), slice(width, width + extra))


def backward(residuals, others, slab, scale):
    units, wide = slab.shape
    width = wide - extra
    near, far = residuals[0].shape[0], residuals[2].shape[0]
    count = near + far
    quarter = units // 8
    sizes = (quarter, quarter, quarter // 2, quarter // 2, quarter) * 2
    vmem = pl.BlockSpec(memory_space=pltpu.VMEM)
    args = (*residuals, *others, slab)
    return pl.pallas_call(
        lambda *refs: backward_kernel(scale, *refs),
        out_shape=tuple(jax.ShapeDtypeStruct((size, wide), jnp.bfloat16) for size in sizes),
        in_specs=[vmem] * len(args),
        out_specs=(vmem,) * len(sizes),
        scratch_shapes=[pltpu.VMEM((units, 1024), jnp.bfloat16), pltpu.VMEM((1024, width), jnp.bfloat16)],
        compiler_params=pltpu.CompilerParams(vmem_limit_bytes=48 * 2**20),
        cost_estimate=pl.CostEstimate(
            flops=12 * count * width * units,
            bytes_accessed=2 * width * (4 * count + 2 * units),
            transcendentals=0,
        ),
    )(*args)


def forward(rows_own, rows_other, slabs, vector=None):
    packed = vector is None
    counts = tuple(slab.shape[0] for slab in slabs)
    units = sum(counts)
    count, width = rows_own.shape
    vmem = pl.BlockSpec(memory_space=pltpu.VMEM)
    sums = jax.ShapeDtypeStruct((count, width), jnp.bfloat16)
    sigmas = jax.ShapeDtypeStruct((count, units), jnp.float32)
    outs = (sums, sums)
    if packed:
        outs += (sigmas, sigmas, jax.ShapeDtypeStruct((units, slabs[0].shape[1]), jnp.bfloat16))
    args = (rows_own, rows_other, *slabs) + (() if packed else (vector,))
    return pl.pallas_call(
        lambda *refs: forward_kernel(counts, packed, *refs),
        out_shape=outs,
        in_specs=[vmem] * 2 + [pl.BlockSpec(memory_space=pl.ANY) if packed else vmem] * (len(args) - 2),
        out_specs=(vmem,) * len(outs),
        scratch_shapes=[pltpu.VMEM((count, units), jnp.bfloat16)] * 2
        + ([pltpu.SemaphoreType.DMA((len(slabs),))] if packed else []),
        compiler_params=pltpu.CompilerParams(vmem_limit_bytes=40 * 2**20),
        cost_estimate=pl.CostEstimate(
            flops=8 * count * width * units,
            bytes_accessed=2 * width * (4 * count + units),
            transcendentals=2 * count * units,
        ),
    )(*args)


def body(
    samples,
    dual_weight,
    dual_vector,
    map_weight,
    map_vector,
    moment_weight,
    square_weight,
    moment_vector,
    square_vector,
):
    core = lax.axis_index("core")
    place = lax.axis_index("z")
    count, width = samples.shape
    inverse_rows = 1.0 / 6144

    packed = jnp.concatenate(
        [
            map_weight.astype(jnp.bfloat16),
            jnp.pad(map_vector.astype(jnp.bfloat16).T, ((0, 0), (0, extra - 2))),
        ],
        axis=1,
    )
    rows_all = lax.all_gather(samples, "z", axis=0, tiled=True)
    half = dual_weight.shape[0] // 2
    dual_half = lax.dynamic_slice_in_dim(dual_weight, core * half, half, axis=0)
    swap = [
        lax.ppermute(dual_half[:96], "xl", flip),
        lax.ppermute(dual_half[96:], "xl", flip),
    ]
    halves = [spread_direct(packed[:16], shift_x), spread_direct(packed[16:], shift_y)]
    pieces, (rows_all, swap[0]) = spread(halves, [shift_y, shift_x], (rows_all, swap[0]))
    rows_own = lax.dynamic_slice_in_dim(
        jnp.concatenate([rows_all, rows_all], axis=0), (place + 6) % 8 * count, 8 * count, axis=0
    )
    rows_other = other_core(rows_own)
    cut = 5 * count

    dual_small = lax.dynamic_slice_in_dim(dual_vector, core * half, half, axis=1)
    dual_small_received = lax.ppermute(dual_small, "xl", flip)
    dual_small_received, rows_own = lax.optimization_barrier((dual_small_received, rows_own))
    dual_pair = jnp.concatenate([dual_small, dual_small_received], axis=1)
    sum_own, sum_other, sigma_own, sigma_other, slab = forward(rows_own, rows_other, pieces)

    def both_cores(own, other):
        return own.astype(jnp.float32) + other_core(other).astype(jnp.float32)

    sample_float = samples.astype(jnp.float32)
    far_sum = both_cores(sum_own[cut:], sum_other[cut:])
    near_sum = both_cores(sum_own[:cut], sum_other[:cut])
    mapped = sample_float + reduce_z(near_sum, far_sum)
    low_near, low_far = gather_z(mapped.astype(jnp.bfloat16))
    dual_slabs = [dual_half, *swap]

    def dual_sum(low):
        return forward(low, other_core(low), dual_slabs, dual_pair)

    dual_near = dual_sum(low_near)
    dual_near, low_far = lax.optimization_barrier((dual_near, low_far))
    dual_far = dual_sum(low_far)
    dual_far = both_cores(*dual_far)
    dual_grad = mapped + reduce_z(both_cores(*dual_near), dual_far)
    residual = (sample_float - dual_grad).astype(jnp.bfloat16)
    residual_near, residual_far = gather_z(residual)

    grads = backward(
        [residual_near, other_core(residual_near), residual_far, other_core(residual_far)],
        [rows_own, rows_other, sigma_own, sigma_other],
        slab,
        inverse_rows,
    )
    across = collect([grads[:5], grads[5:]], [shift_y, shift_x])
    grad_first = collect_direct(across[0], shift_x)
    grad_second = collect_direct(across[1], shift_y)
    owner = jnp.concatenate([grad_first, grad_second], axis=0)
    owner_weight = owner[:, :width]
    owner_vector = owner[:, width : width + 2].T

    next_weight, next_moment_weight, next_square_weight = adam_update(
        map_weight, owner_weight, moment_weight, square_weight
    )
    raw_vector, next_moment_vector, next_square_vector = adam_update(
        map_vector, owner_vector, moment_vector, square_vector
    )
    next_vector = jnp.concatenate([jnp.maximum(raw_vector[0:1], 0.0), raw_vector[1:2]], axis=0)
    return (
        next_weight,
        next_vector,
        next_moment_weight,
        next_square_weight,
        next_moment_vector,
        next_square_vector,
    )


def solution(mesh):
    fsdp = ("xl", "z")
    rep = ("y", "xh", "core")
    fine = Mesh(mesh.devices.reshape(2, 8, 4, 2, 2), fsdp + rep)
    rows = P(fsdp + rep, None)
    columns = P(None, fsdp + rep)
    return jax.shard_map(
        body,
        mesh=fine,
        in_specs=(rows, P(fsdp, None), P(None, fsdp), rows, columns, rows, rows, columns, columns),
        out_specs=(rows, columns, rows, rows, columns, columns),
        check_vma=False,
    )
```

```python
import jax
import jax.numpy as jnp
from jax import lax
from jax.experimental import pallas as pl
from jax.experimental.pallas import tpu as pltpu
from jax.sharding import Mesh, PartitionSpec as P

beta_one = 0.9
beta_two = 0.999
learn_rate = 0.001
epsilon = 1e-08
adam_step = 10
extra = 128

flip = [(0, 1), (1, 0)]


def contract_last(left, right):
    return lax.dot_general(
        left, right, (((1,), (1,)), ((), ())), preferred_element_type=jnp.float32
    )


def contract_first(left, right):
    return lax.dot_general(
        left, right, (((0,), (0,)), ((), ())), preferred_element_type=jnp.float32
    )


def dot(left, right):
    return jnp.dot(left, right, preferred_element_type=jnp.float32)


def adam_update(param, grad, moment, square):
    moment_new = beta_one * moment + (1.0 - beta_one) * grad
    square_new = beta_two * square + (1.0 - beta_two) * grad * grad
    fix_one = 1.0 - beta_one**adam_step
    fix_two = 1.0 - beta_two**adam_step
    update = learn_rate * (moment_new / fix_one) / (jnp.sqrt(square_new / fix_two) + epsilon)
    return (param - update, moment_new, square_new)


def shift_y(value, step):
    return lax.ppermute(value, "y", [(i, (i + step) % 4) for i in range(4)])


ring_x = (0, 2, 1, 3)


def shift_x(value, step):
    return lax.ppermute(
        value, ("xl", "xh"), [(ring_x[i], ring_x[(i + step) % 4]) for i in range(4)]
    )


def spread_direct(value, shift):
    return jnp.concatenate([value] + [shift(value, step) for step in (1, 2, 3)], axis=0)


def collect_direct(value, shift):
    rows = value.shape[0] // 4
    low = value.astype(jnp.bfloat16)
    total = value[:rows]
    for step in (1, 2, 3):
        total = total + shift(low[rows * step : rows * (step + 1)], -step).astype(jnp.float32)
    return total


def spread(parts, shifts, ride):
    half = parts[0].shape[0] // 2
    sent = [shift(value, step) for value, shift in zip(parts, shifts) for step in (1, -1)]
    sent = lax.optimization_barrier(sent)
    again = [shifts[0](sent[0][:half], 1), shifts[0](sent[1][half:], -1)]
    sent[2:], again, ride = lax.optimization_barrier((sent[2:], again, ride))
    again += [shifts[1](sent[2][:half], 1), shifts[1](sent[3][half:], -1)]
    pieces = []
    for i, value in enumerate(parts):
        pieces += [value, sent[2 * i], again[2 * i], again[2 * i + 1], sent[2 * i + 1]]
    return pieces, ride


def collect(parts, shifts):
    wide, low = jnp.float32, jnp.bfloat16
    sent = []
    for (_, _, front, back, _), shift in zip(parts, shifts):
        sent += [shift(front, -1), shift(back, 1)]
    sent = lax.optimization_barrier(sent)
    half = sent[0].shape[0]
    final = []
    for index, ((_, behind, _, _, ahead), shift) in enumerate(zip(parts, shifts)):
        front, back = sent[2 * index].astype(wide), sent[2 * index + 1].astype(wide)
        behind = jnp.concatenate([(behind[:half].astype(wide) + front).astype(low), behind[half:]])
        ahead = jnp.concatenate([ahead[:half], (ahead[half:].astype(wide) + back).astype(low)])
        final += [shift(behind, -1), shift(ahead, 1)]
    final = lax.optimization_barrier(final)
    return [
        own[0].astype(wide) + final[2 * i].astype(wide) + final[2 * i + 1].astype(wide)
        for i, own in enumerate(parts)
    ]


def other_core(value):
    return lax.ppermute(value, "core", flip)


def shift_z(value, step):
    return lax.ppermute(value, "z", [(i, (i + step) % 8) for i in range(8)])


def gather_z(value):
    middle = value.shape[1] // 2
    from_ahead, from_behind = shift_z(value, -2), shift_z(value, 2)
    next_ahead, next_behind = shift_z(value, -1), shift_z(value, 1)
    left, right = shift_z(from_behind[:, :middle], 2), shift_z(from_ahead[:, middle:], -2)
    third_ahead, third_behind = shift_z(from_ahead, -1), shift_z(from_behind, 1)
    return (
        jnp.concatenate([from_behind, next_behind, value, next_ahead, from_ahead], axis=0),
        jnp.concatenate(
            [third_ahead, jnp.concatenate([left, right], axis=1), third_behind], axis=0
        ),
    )


def reduce_z(near_sum, far_sum):
    wide = jnp.float32
    count = near_sum.shape[0] // 5
    middle = near_sum.shape[1] // 2

    def near_block(index):
        return near_sum[count * (index + 2) : count * (index + 3)]

    third_ahead, fourth, third_behind = (far_sum[count * i : count * (i + 1)] for i in range(3))
    low = jnp.bfloat16
    left = shift_z(fourth[:, :middle].astype(low), 2)
    right = shift_z(fourth[:, middle:].astype(low), -2)
    ahead = shift_z(third_ahead.astype(low), 1)
    behind = shift_z(third_behind.astype(low), -1)
    beside_ahead = shift_z(near_block(1).astype(low), 1)
    beside_behind = shift_z(near_block(-1).astype(low), -1)
    ahead_sum = near_block(2).astype(wide) + ahead.astype(wide)
    behind_sum = near_block(-2).astype(wide) + behind.astype(wide)
    ahead_sum = jnp.concatenate(
        [ahead_sum[:, :middle] + left.astype(wide), ahead_sum[:, middle:]], axis=1
    )
    behind_sum = jnp.concatenate(
        [behind_sum[:, :middle], behind_sum[:, middle:] + right.astype(wide)], axis=1
    )
    from_behind = shift_z(ahead_sum.astype(low), 2)
    from_ahead = shift_z(behind_sum.astype(low), -2)
    total = near_block(0).astype(wide) + beside_ahead.astype(wide) + beside_behind.astype(wide)
    return total + from_behind.astype(wide) + from_ahead.astype(wide)


tile = 512


def forward_kernel(counts, packed, *refs):
    own_ref, other_ref = refs[:2]
    slabs = refs[2 : 2 + len(counts)]
    refs = refs[2 + len(counts) :]
    if packed:
        slab, begin, copies = refs[4], 0, []
        for index, (piece, count) in enumerate(zip(slabs, counts)):
            target = slab.at[begin : begin + count]
            copies.append(pltpu.make_async_copy(piece, target, refs[7].at[index]))
            begin += count
        for copy in copies:
            copy.start()
        for copy in copies:
            copy.wait()
        slabs, counts = [slab], [begin]
        tail = slab[:, own_ref.shape[1] :]
        vector = contract_last(pick_rows(), tail)
        readout, offset = vector[0:1], vector[1:2]
        sum_refs, sigma_refs = refs[0:2], refs[2:4]
        scratch = refs[5:7]
    else:
        readout, offset = refs[0][0:1], refs[0][1:2]
        sum_refs, sigma_refs = refs[1:3], None
        scratch = refs[3:]
    width = own_ref.shape[1]
    for index, rows in enumerate((own_ref, other_ref)):
        begin = 0
        for slab, count in zip(slabs, counts):
            for low in range(0, count, 256):
                size = min(256, count - low)
                hidden = contract_last(rows[...], slab[low : low + size, :width])
                span = slice(begin + low, begin + low + size)
                sigma = jax.nn.sigmoid(hidden + offset[:, span])
                if sigma_refs is not None:
                    sigma_refs[index][:, span] = sigma
                scratch[index][:, span] = (readout[:, span] * sigma).astype(jnp.bfloat16)
            begin += count

    @pl.loop(0, width // tile)
    def _(step):
        columns = pl.ds(pl.multiple_of(step * tile, tile), tile)
        for index in (1, 0):
            total, begin = None, 0
            for slab, count in zip(slabs, counts):
                part = dot(scratch[index][:, begin : begin + count], slab[:, columns])
                total = part if total is None else total + part
                begin += count
            sum_refs[index][:, columns] = total.astype(jnp.bfloat16)


def pick_rows():
    lane = lax.broadcasted_iota(jnp.int32, (8, extra), 1)
    row = lax.broadcasted_iota(jnp.int32, (8, extra), 0)
    return jnp.where(lane == row, 1.0, 0.0).astype(jnp.bfloat16)


def backward_kernel(scale, *refs):
    near_refs, far_refs = refs[0:2], refs[2:4]
    rows_refs, sigma_refs, slab = refs[4:6], refs[6:8], refs[8]
    out_refs, left, right = refs[9:-2], refs[-2], refs[-1]
    units = slab.shape[0]
    count, width = rows_refs[0].shape
    cut = near_refs[0].shape[0]
    readout = contract_last(pick_rows(), slab[:, width:])[0:1]
    none = jnp.bfloat16(0.0)
    starts = ((0, 512, 768), (256, 640, 896))
    for index in range(2):
        for begin, ref in zip(starts[index], (rows_refs[index], near_refs[index], far_refs[index])):
            size = ref.shape[0]
            room, whole = (256 if size > 128 else 128), size // 16 * 16
            right[begin + whole : begin + room] = jnp.full((room - whole, width), none)
            right[begin : begin + size] = ref[...]
            left[:, begin + room - 128 : begin + room] = jnp.full((units, 128), none)
    sums = []
    for index in range(2):
        for low in range(0, units, 256):
            span = slice(low, low + 256)
            factor = readout[:, span]
            near = contract_last(near_refs[index][...], slab[span, :width])
            far = contract_last(far_refs[index][...], slab[span, :width])
            pulled = jnp.concatenate([near, far], axis=0)
            sigma = sigma_refs[index][:, span]
            scaled = factor * sigma
            curve = scaled * (1.0 - sigma) * pulled
            parts = (curve, scaled[:cut], scaled[cut:])
            for begin, part in zip(starts[index], parts):
                left[span, begin : begin + part.shape[0]] = jnp.transpose(part).astype(jnp.bfloat16)
            pair = (jnp.sum(sigma * pulled, axis=0), jnp.sum(curve, axis=0))
            if index == 0:
                sums.append(pair)
            else:
                old = sums[low // 256]
                sums[low // 256] = (old[0] + pair[0], old[1] + pair[1])

    def store(total, columns):
        begin = 0
        for ref in out_refs:
            ref[:, columns] = total[begin : begin + ref.shape[0]].astype(jnp.bfloat16)
            begin += ref.shape[0]

    @pl.loop(0, width // tile)
    def _(step):
        columns = pl.ds(pl.multiple_of(step * tile, tile), tile)
        total = dot(left[...], right[:, columns])
        store(total * scale, columns)

    row = lax.broadcasted_iota(jnp.int32, (8, 256), 0)
    small = [jnp.where(row == 0, a[None], jnp.where(row == 1, b[None], 0.0)) for a, b in sums]
    small = (jnp.concatenate(small, axis=1) * scale).astype(jnp.bfloat16)
    store(contract_first(small, pick_rows()), slice(width, width + extra))


def backward(residuals, others, slab, scale):
    units, wide = slab.shape
    width = wide - extra
    near, far = residuals[0].shape[0], residuals[2].shape[0]
    count = near + far
    quarter = units // 8
    sizes = (quarter, quarter, quarter // 2, quarter // 2, quarter) * 2
    vmem = pl.BlockSpec(memory_space=pltpu.VMEM)
    args = (*residuals, *others, slab)
    return pl.pallas_call(
        lambda *refs: backward_kernel(scale, *refs),
        out_shape=tuple(jax.ShapeDtypeStruct((size, wide), jnp.bfloat16) for size in sizes),
        in_specs=[vmem] * len(args),
        out_specs=(vmem,) * len(sizes),
        scratch_shapes=[pltpu.VMEM((units, 1024), jnp.bfloat16), pltpu.VMEM((1024, width), jnp.bfloat16)],
        compiler_params=pltpu.CompilerParams(vmem_limit_bytes=48 * 2**20),
        cost_estimate=pl.CostEstimate(
            flops=12 * count * width * units,
            bytes_accessed=2 * width * (4 * count + 2 * units),
            transcendentals=0,
        ),
    )(*args)


def forward(rows_own, rows_other, slabs, vector=None):
    packed = vector is None
    counts = tuple(slab.shape[0] for slab in slabs)
    units = sum(counts)
    count, width = rows_own.shape
    vmem = pl.BlockSpec(memory_space=pltpu.VMEM)
    sums = jax.ShapeDtypeStruct((count, width), jnp.bfloat16)
    sigmas = jax.ShapeDtypeStruct((count, units), jnp.float32)
    outs = (sums, sums)
    if packed:
        outs += (sigmas, sigmas, jax.ShapeDtypeStruct((units, slabs[0].shape[1]), jnp.bfloat16))
    args = (rows_own, rows_other, *slabs) + (() if packed else (vector,))
    return pl.pallas_call(
        lambda *refs: forward_kernel(counts, packed, *refs),
        out_shape=outs,
        in_specs=[vmem] * 2 + [pl.BlockSpec(memory_space=pl.ANY) if packed else vmem] * (len(args) - 2),
        out_specs=(vmem,) * len(outs),
        scratch_shapes=[pltpu.VMEM((count, units), jnp.bfloat16)] * 2
        + ([pltpu.SemaphoreType.DMA((len(slabs),))] if packed else []),
        compiler_params=pltpu.CompilerParams(vmem_limit_bytes=40 * 2**20),
        cost_estimate=pl.CostEstimate(
            flops=8 * count * width * units,
            bytes_accessed=2 * width * (4 * count + units),
            transcendentals=2 * count * units,
        ),
    )(*args)


def body(
    samples,
    dual_weight,
    dual_vector,
    map_weight,
    map_vector,
    moment_weight,
    square_weight,
    moment_vector,
    square_vector,
):
    core = lax.axis_index("core")
    place = lax.axis_index("z")
    count, width = samples.shape
    inverse_rows = 1.0 / 6144

    packed = jnp.concatenate(
        [
            map_weight.astype(jnp.bfloat16),
            jnp.pad(map_vector.astype(jnp.bfloat16).T, ((0, 0), (0, extra - 2))),
        ],
        axis=1,
    )
    rows_all = lax.all_gather(samples, "z", axis=0, tiled=True)
    half = dual_weight.shape[0] // 2
    dual_half = lax.dynamic_slice_in_dim(dual_weight, core * half, half, axis=0)
    swap = [
        lax.ppermute(dual_half[:96], "xl", flip),
        lax.ppermute(dual_half[96:], "xl", flip),
    ]
    halves = [spread_direct(packed[:16], shift_x), spread_direct(packed[16:], shift_y)]
    pieces, (rows_all, swap[0]) = spread(halves, [shift_y, shift_x], (rows_all, swap[0]))
    rows_own = lax.dynamic_slice_in_dim(
        jnp.concatenate([rows_all, rows_all], axis=0), (place + 6) % 8 * count, 8 * count, axis=0
    )
    rows_other = other_core(rows_own)
    cut = 5 * count

    dual_small = lax.dynamic_slice_in_dim(dual_vector, core * half, half, axis=1)
    dual_small_received = lax.ppermute(dual_small, "xl", flip)
    dual_small_received, rows_own = lax.optimization_barrier((dual_small_received, rows_own))
    dual_pair = jnp.concatenate([dual_small, dual_small_received], axis=1)
    sum_own, sum_other, sigma_own, sigma_other, slab = forward(rows_own, rows_other, pieces)

    def both_cores(own, other):
        return own.astype(jnp.float32) + other_core(other).astype(jnp.float32)

    sample_float = samples.astype(jnp.float32)
    far_sum = both_cores(sum_own[cut:], sum_other[cut:])
    near_sum = both_cores(sum_own[:cut], sum_other[:cut])
    mapped = sample_float + reduce_z(near_sum, far_sum)
    low_near, low_far = gather_z(mapped.astype(jnp.bfloat16))
    dual_slabs = [dual_half, *swap]

    def dual_sum(low):
        return forward(low, other_core(low), dual_slabs, dual_pair)

    dual_near = dual_sum(low_near)
    dual_near, low_far = lax.optimization_barrier((dual_near, low_far))
    dual_far = dual_sum(low_far)
    dual_far = both_cores(*dual_far)
    dual_grad = mapped + reduce_z(both_cores(*dual_near), dual_far)
    residual = (sample_float - dual_grad).astype(jnp.bfloat16)
    residual_near, residual_far = gather_z(residual)

    grads = backward(
        [residual_near, other_core(residual_near), residual_far, other_core(residual_far)],
        [rows_own, rows_other, sigma_own, sigma_other],
        slab,
        inverse_rows,
    )
    across = collect([grads[:5], grads[5:]], [shift_y, shift_x])
    grad_first = collect_direct(across[0], shift_x)
    grad_second = collect_direct(across[1], shift_y)
    owner = jnp.concatenate([grad_first, grad_second], axis=0)
    owner_weight = owner[:, :width]
    owner_vector = owner[:, width : width + 2].T

    next_weight, next_moment_weight, next_square_weight = adam_update(
        map_weight, owner_weight, moment_weight, square_weight
    )
    raw_vector, next_moment_vector, next_square_vector = adam_update(
        map_vector, owner_vector, moment_vector, square_vector
    )
    next_vector = jnp.concatenate([jnp.maximum(raw_vector[0:1], 0.0), raw_vector[1:2]], axis=0)
    return (
        next_weight,
        next_vector,
        next_moment_weight,
        next_square_weight,
        next_moment_vector,
        next_square_vector,
    )


def solution(mesh):
    fsdp = ("xl", "z")
    rep = ("y", "xh", "core")
    fine = Mesh(mesh.devices.reshape(2, 8, 4, 2, 2), fsdp + rep)
    rows = P(fsdp + rep, None)
    columns = P(None, fsdp + rep)
    return jax.shard_map(
        body,
        mesh=fine,
        in_specs=(rows, P(fsdp, None), P(None, fsdp), rows, columns, rows, rows, columns, columns),
        out_specs=(rows, columns, rows, rows, columns, columns),
        check_vma=False,
    )
```
